128 devices in a mesh: dp: 16 (over z_lo, y, core), seq: 8 (over z_hi, x).
Axes of the slice: x: 4, y: 4, z: 4 (z_hi: 2, z_lo: 2; z = z_hi * 2 + z_lo), core: 2. Of those that a mesh axis runs over, the one named last changes fastest.
Arguments:
- hidden: bfloat16 [32768, 1536], P(('dp', 'seq')), may hold values from -24 to 24
- masked: int32 [32768], P(('dp', 'seq')), may hold values 0 or 1
- clip_lengths: int32 [16, 3], P('dp'), may hold values from 1 to 1024, 2048 in all within a row
- qkv_weight: bfloat16 [1536, 2304], replicated, may hold values from -0.5 to 0.5
- cotangent: bfloat16 [32768, 768], P(('dp', 'seq')), may hold values from -6 to 6
Outputs:
- attn_out: bfloat16 [32768, 768], P(('dp', 'seq'))
- weight_grad: float32 [1536, 2304], P(('dp', 'seq'))
The draws below stay inside these ranges and needn't reach their ends.
Inputs may be any that keep to these rules, and one draw needn't show every extreme that they name: Each row of clip_lengths sums to 2048, and its longest clip has exactly 1024 tokens.
All inputs are finite; a program needn't handle non-finite values. No bound on the sum of `masked` on one device may be relied on, other than what follows from the above.
Results may differ from the reference program's by a relative error of at most 0.017.
Values may be sent and summed in bfloat16 or wider, within the bound.
A program may use at most 192 MiB of HBM per device.

```python
import math
import jax
import jax.numpy as jnp
import numpy as np
from jax import lax

D = 1536
HEADS = 12
HSIZE = 64
CLIPS = 3
GROUP = 2048
TOKENS = 32768
N_DP = 16


def draw_qkv_weight(key, part):
    key = jax.random.fold_in(key, 7)
    width = HEADS * HSIZE
    base = jax.random.normal(key, (D, 3 * width), jnp.float32) * D ** (-0.5)
    return jnp.clip(base, -0.5, 0.5).astype(jnp.bfloat16)


def place_ends(drawn, key, low, top_value):
    shape = drawn.shape
    index_at = [jax.random.randint(jax.random.fold_in(key, axis), (), 0, shape[axis]) for axis in range(len(shape))]
    drawn = drawn.at[tuple(index_at)].set(low)
    longest = shape.index(max(shape))
    index_at[longest] = (index_at[longest] + 1) % shape[longest]
    return drawn.at[tuple(index_at)].set(top_value)


def raised(array, stream_key, source, target, blocks, factor):
    owner, partner = [(jnp.arange(array.shape[dim]) // (array.shape[dim] // blocks)).reshape([-1 if axis == dim else 1 for axis in range(array.ndim)]) for dim in (source, target)]
    chosen = jax.random.permutation(stream_key, blocks)[partner]
    strong = (owner == chosen) | (owner == (partner + blocks // 2) % blocks)
    return jnp.where(strong, factor * array, array)


def levels(key, extent, shards, smallest, high):
    factor_of, own = 1.0, jax.random.fold_in(key, 6)
    for dim, shards_of in shards:
        steps = jnp.exp(jax.random.uniform(jax.random.fold_in(own, dim), (shards_of,), jnp.float32, smallest / len(shards), high / len(shards)))
        factor_of = factor_of * jnp.repeat(steps, extent[dim] // shards_of).reshape([-1 if axis == dim else 1 for axis in range(len(extent))])
    return factor_of


def profile(number_of, total, most, lean):
    portions = [(1 << 20) // math.isqrt(grade ** lean) + 1 for grade in range(2, number_of + 1)]
    spare, counts = total - most - (number_of - 1), [1] * (number_of - 1)
    while spare > 0:
        free = [i for i in range(number_of - 1) if counts[i] < most]
        pool, budget = sum([portions[i] for i in free]), spare
        for i in free:
            addition = min(most - counts[i], max(1, budget * portions[i] // pool), spare)
            counts[i] = counts[i] + addition
            spare = spare - addition
    return np.array([most] + counts)


def ragged_sizes(own_key, amount, total, limit, lean):
    if amount == 2:
        one = jax.random.randint(own_key, (), max(1, total - limit), min(limit, total - 1) + 1)
        return jnp.stack([one, total - one])
    tallies = jnp.asarray(profile(amount, total, limit, lean), jnp.int32)
    twos = (amount - 1) // 2
    giver, receiver = tallies[1:1 + 2 * twos:2], tallies[2:2 + 2 * twos:2]
    room = jnp.minimum(giver - 1, limit - receiver)
    shifted = jax.random.randint(jax.random.fold_in(own_key, 1), (twos,), 0, 1 << 20) % (room + 1)
    tallies = tallies.at[1:1 + 2 * twos:2].set(giver - shifted).at[2:2 + 2 * twos:2].set(receiver + shifted)
    return tallies[jax.random.permutation(jax.random.fold_in(own_key, 2), amount)]


def scatter_about(key, extent, deviation, bound, cuts=(), kind=jnp.bfloat16):
    values = deviation * jax.random.normal(key, extent, jnp.float32)
    if cuts:
        values = values * levels(key, extent, cuts, -0.22, 0.18)
    return jnp.clip(values, -bound, bound).astype(kind)


def bell_draw_with(stream_key, extent, spread, reach, pieces, heavy, held_as=jnp.bfloat16):
    drawn = spread * jax.random.normal(stream_key, extent, jnp.float32)
    if pieces:
        drawn = drawn * levels(stream_key, extent, pieces, -0.22, 0.18)
    return jnp.clip(raised(drawn, jax.random.fold_in(stream_key, 3), *heavy), -reach, reach).astype(held_as)


def setup_inputs(seed: int = 0) -> dict:
    arg_keys = jax.random.split(jax.random.key(seed), 6)
    return {
        "hidden": bell_draw_with(arg_keys[0], (TOKENS, D), 1.0, 24.0, ((0, 128),), (0, 1, 128, 5.5)),
        "masked": place_ends((jax.random.randint(arg_keys[1], (TOKENS,), 0, 2) < 1).astype(jnp.int32), jax.random.fold_in(arg_keys[1], 1), 0, 1),
        "clip_lengths": jax.vmap(lambda own: ragged_sizes(own, CLIPS, GROUP, GROUP // 2, 2))(jax.random.split(arg_keys[2], N_DP)).reshape((N_DP, CLIPS)).astype(jnp.int32),
        "qkv_weight": draw_qkv_weight(jax.random.fold_in(arg_keys[5], 71), 0),
        "cotangent": scatter_about(arg_keys[4], (TOKENS, HEADS * HSIZE), 1.0, 6.0, ((0, 128),)),
    }


neg_fill = -1e+30
score_scale = 0.125

def segment_ids(lengths, first_row, row_span):
    clip_ends = jnp.cumsum(lengths)
    position = first_row + jnp.arange(row_span, dtype=jnp.int32)
    return lax.optimization_barrier(jnp.sum((position[:, None] >= clip_ends[None, :]).astype(jnp.int32), axis=1))

def rms_rows(hidden):
    widened = hidden.astype(jnp.float32)
    scale_rows = lax.rsqrt(lax.optimization_barrier(jnp.mean(widened * widened, axis=1, keepdims=True)) + 1e-06)
    return (widened * scale_rows).astype(jnp.bfloat16)

def head_major(matrix, head_count):
    return matrix.reshape(matrix.shape[0], head_count, -1).transpose(1, 0, 2)

def reference(hidden, masked, clip_lengths, qkv_weight, cotangent):
    group = GROUP
    width = HEADS * HSIZE

    def token_major(stacked):
        return stacked.transpose(1, 0, 2).reshape(group, width)

    def one_group(grad_sum, items):
        rows_in, mask_in, lengths, cot_in = items
        normed = rms_rows(rows_in)
        qkv = jnp.dot(normed, qkv_weight, preferred_element_type=jnp.float32).astype(jnp.bfloat16)
        segment = segment_ids(lengths, 0, group)
        same_clip = segment[:, None] == segment[None, :]
        upstream = jnp.where(mask_in[:, None] == 1, cot_in, jnp.zeros_like(cot_in))

        def one_head(slices):
            queries, keys_in, values, grads_in = slices
            scores = jnp.dot(queries, keys_in.T, preferred_element_type=jnp.float32) * score_scale
            scores = jnp.where(same_clip, scores, neg_fill)
            maxima = lax.optimization_barrier(jnp.max(scores, axis=1, keepdims=True))
            weights = jnp.where(same_clip, jnp.exp(scores - maxima), 0.0)
            totals = lax.optimization_barrier(jnp.sum(weights, axis=1, keepdims=True))
            output = (jnp.dot(weights.astype(jnp.bfloat16), values, preferred_element_type=jnp.float32) / totals).astype(jnp.bfloat16)
            delta = lax.optimization_barrier(jnp.sum(grads_in.astype(jnp.float32) * output.astype(jnp.float32), axis=1, keepdims=True))
            probability = weights / totals
            dprob = jnp.dot(grads_in, values.T, preferred_element_type=jnp.float32)
            score_grad = (probability * (dprob - delta)).astype(jnp.bfloat16)
            query_grad = (jnp.dot(score_grad, keys_in, preferred_element_type=jnp.float32) * score_scale).astype(jnp.bfloat16)
            key_grad = (jnp.dot(score_grad.T, queries, preferred_element_type=jnp.float32) * score_scale).astype(jnp.bfloat16)
            value_grad = jnp.dot(probability.astype(jnp.bfloat16).T, grads_in, preferred_element_type=jnp.float32).astype(jnp.bfloat16)
            return (output, query_grad, key_grad, value_grad)
        stacked = (head_major(qkv[:, :width], HEADS), head_major(qkv[:, width:2 * width], HEADS), head_major(qkv[:, 2 * width:], HEADS), head_major(upstream, HEADS))
        output, query_grad, key_grad, value_grad = lax.map(one_head, stacked)
        grads_all = jnp.concatenate([token_major(query_grad), token_major(key_grad), token_major(value_grad)], axis=1)
        grad_sum = grad_sum + jnp.dot(normed.T, grads_all, preferred_element_type=jnp.float32)
        return (grad_sum, token_major(output))
    items = (hidden.reshape(N_DP, group, D), masked.reshape(N_DP, group), clip_lengths, cotangent.reshape(N_DP, group, width))
    start_grad = jnp.zeros((D, 3 * width), jnp.float32)
    weight_grad, outputs = lax.scan(one_group, start_grad, items)
    return (outputs.reshape(TOKENS, width), weight_grad)
```

```python
import functools

import jax
import jax.numpy as jnp
from jax import lax
from jax.experimental import pallas as pl
from jax.experimental.pallas import tpu as pltpu
from jax.sharding import PartitionSpec as P

MESH = pl.DeviceIdType.MESH
VMEM = pltpu.VMEM
HS = 64
NH = 3
GW = NH * HS
BLK = 256
D = 1536
WIDTH = 768
NEG = -1e30
SCALE = 0.125
LIMIT = 60 * 1024 * 1024


def coords():
    dp = lax.axis_index("dp")
    sq = lax.axis_index("seq")
    core = lax.rem(dp, 2)
    y = lax.rem(dp // 2, 4)
    zl = dp // 8
    x = lax.rem(sq, 4)
    zh = sq // 4
    return x, y, zh, zl, core


def dev(x, y, zh, zl, core):
    return ((zl * 4 + y) * 2 + core, zh * 4 + x)


def mod4(v):
    return lax.rem(v, 4)


def greet(partners):
    barrier = pltpu.get_barrier_semaphore()
    for p in partners:
        pl.semaphore_signal(barrier, inc=1, device_id=p, device_id_type=MESH)
    pl.semaphore_wait(barrier, len(partners))


def dot(a, b):
    return jnp.dot(a, b, preferred_element_type=jnp.float32)


def dot_nt(a, b):
    return lax.dot_general(a, b, (((1,), (1,)), ((), ())), preferred_element_type=jnp.float32)


def project_kernel(
    hidden_ref, mask_ref, cot_ref, w_ref,
    qt_ref, ut_ref, kv_ref, nt_ref,
    land, wbuf, usend, wsem, ssem, rsem, zs, zr, us, ur,
):
    x, y, zh, zl, core = coords()
    right = dev(mod4(x + 1), y, zh, zl, core)
    left = dev(mod4(x + 3), y, zh, zl, core)
    far = dev(mod4(x + 2), y, zh, zl, core)
    zp = dev(x, y, 1 - zh, zl, core)
    lane0 = (3 * x) // 2 * 128
    odd = lax.rem(x, 2) == 1

    wcopies = []
    for j in range(3):
        c = pltpu.make_async_copy(
            w_ref.at[:, pl.ds(pl.multiple_of(WIDTH * j + lane0, 128), 256)], wbuf.at[j], wsem.at[j]
        )
        c.start()
        wcopies.append(c)
    greet([right, left, far, zp])

    half = BLK // 2
    top, bot = pl.ds(0, half), pl.ds(half, half)

    def rcopy(src, dst, i, to):
        return pltpu.make_async_remote_copy(
            src_ref=src, dst_ref=dst, send_sem=ssem.at[i], recv_sem=rsem.at[i],
            device_id=to, device_id_type=MESH,
        )

    a0 = rcopy(hidden_ref.at[top], land.at[0, top], 0, right)
    a1 = rcopy(hidden_ref.at[bot], land.at[1, bot], 1, left)
    a2 = rcopy(hidden_ref.at[bot], land.at[0, bot], 2, right)
    a3 = rcopy(hidden_ref.at[top], land.at[1, top], 3, left)
    for c in (a0, a1, a2, a3):
        c.start()
    b0 = rcopy(land.at[0, top], land.at[2, top], 4, right)
    b1 = rcopy(land.at[1, bot], land.at[2, bot], 5, left)

    upstream = jnp.where(mask_ref[...] == 1, cot_ref[...].astype(jnp.float32), 0.0)
    for g in range(4):
        usend[g] = upstream[:, GW * g : GW * (g + 1)].T.astype(jnp.bfloat16)
    for c in wcopies:
        c.wait()

    def pick(r):
        return jnp.where(odd, r[:, 64:256], r[:, 0:192])

    def process(h, xb):
        h = h.astype(jnp.float32)
        scale = lax.rsqrt(jnp.mean(h * h, axis=1, keepdims=True) + 1e-06)
        normed = (h * scale).astype(jnp.bfloat16)
        q = pick(dot(normed, wbuf[0])).astype(jnp.bfloat16).astype(jnp.float32)
        qt_ref[xb] = (q * SCALE).T.astype(jnp.bfloat16)
        k = pick(dot(normed, wbuf[1]))
        v = pick(dot(normed, wbuf[2]))
        kv_ref[zh * 4 + xb] = jnp.concatenate([k, v], axis=1).astype(jnp.bfloat16)
        c = pltpu.make_async_remote_copy(
            src_ref=kv_ref.at[zh * 4 + xb], dst_ref=kv_ref.at[zh * 4 + xb],
            send_sem=zs.at[xb], recv_sem=zr.at[xb], device_id=zp, device_id_type=MESH,
        )
        c.start()
        nt = normed.T
        lanes = pl.ds(pl.multiple_of(xb * BLK, BLK), BLK)
        for j in range(8):
            for c2 in range(2):
                nt_ref[c2, 96 * j : 96 * (j + 1), lanes] = nt[192 * j + 96 * c2 : 192 * j + 96 * (c2 + 1), :]

    process(hidden_ref[...], x)
    a0.wait_recv()
    b0.start()
    a1.wait_recv()
    b1.start()
    ucopies = []
    for d, to in ((1, right), (2, far), (3, left)):
        c = pltpu.make_async_remote_copy(
            src_ref=usend.at[mod4(x + d)], dst_ref=ut_ref.at[x],
            send_sem=us.at[d - 1], recv_sem=ur.at[d - 1], device_id=to, device_id_type=MESH,
        )
        c.start()
        ucopies.append(c)
    ut_ref[x] = usend[x]
    a2.wait_recv()
    process(land[0], mod4(x + 3))
    a3.wait_recv()
    process(land[1], mod4(x + 1))
    b0.wait_recv()
    b1.wait_recv()
    process(land[2], mod4(x + 2))
    for c in (a0, a1, a2, a3, b0, b1):
        c.wait_send()
    for c in ucopies:
        c.wait()
    for xb in range(4):
        ours, theirs = zh * 4 + xb, (1 - zh) * 4 + xb
        pltpu.make_async_remote_copy(
            src_ref=kv_ref.at[ours], dst_ref=kv_ref.at[ours], send_sem=zs.at[xb], recv_sem=zr.at[xb],
            device_id=zp, device_id_type=MESH,
        ).wait_send()
        pltpu.make_async_remote_copy(
            src_ref=kv_ref.at[theirs], dst_ref=kv_ref.at[theirs], send_sem=zs.at[xb], recv_sem=zr.at[xb],
            device_id=zp, device_id_type=MESH,
        ).wait_recv()


def project(hidden, mask, cot, w):
    bf = jnp.bfloat16
    return pl.pallas_call(
        project_kernel,
        out_shape=(
            jax.ShapeDtypeStruct((4, GW, BLK), bf),
            jax.ShapeDtypeStruct((4, GW, BLK), bf),
            jax.ShapeDtypeStruct((8, BLK, 2 * GW), bf),
            jax.ShapeDtypeStruct((2, WIDTH, 4 * BLK), bf),
        ),
        in_specs=[pl.BlockSpec(memory_space=VMEM)] * 3 + [pl.BlockSpec(memory_space=pl.ANY)],
        out_specs=[pl.BlockSpec(memory_space=VMEM)] * 4,
        scratch_shapes=[
            VMEM((3, BLK, D), bf),
            VMEM((3, D, 256), bf),
            VMEM((4, GW, BLK), bf),
            pltpu.SemaphoreType.DMA((3,)),
            pltpu.SemaphoreType.DMA((6,)),
            pltpu.SemaphoreType.DMA((6,)),
            pltpu.SemaphoreType.DMA((4,)),
            pltpu.SemaphoreType.DMA((4,)),
            pltpu.SemaphoreType.DMA((3,)),
            pltpu.SemaphoreType.DMA((3,)),
        ],
        compiler_params=pltpu.CompilerParams(collective_id=0, has_side_effects=True, vmem_limit_bytes=LIMIT),
        name="project",
    )(hidden, mask, cot, w)


def attend_kernel(
    sc_ref, qt_ref, ut_ref, kv_ref, outt_ref, qg_ref, kvg_ref, s_scr, p_scr, kvt, acc, ot, gt
):
    e0, e1, base = sc_ref[0], sc_ref[1], sc_ref[2]
    CH = 256
    acc[...] = jnp.zeros_like(acc)
    for c in range(8):
        kvt[:, CH * c : CH * (c + 1)] = kv_ref[CH * c : CH * (c + 1), :].T

    def segment(pos):
        return (pos >= e0).astype(jnp.int32) + (pos >= e1).astype(jnp.int32)

    @pl.loop(0, 4)
    def _(i):
        r0 = base + BLK * i
        r1 = r0 + BLK - 1
        low = jnp.where(r0 >= e1, e1, jnp.where(r0 >= e0, e0, 0))
        high = jnp.where(r1 < e0, e0, jnp.where(r1 < e1, e1, 2048))
        c0 = low // CH
        c1 = (high + CH - 1) // CH
        qseg = segment(r0 + lax.broadcasted_iota(jnp.int32, (1, BLK), 1))

        def pass1(c, ms):
            rows = pl.ds(pl.multiple_of(c * CH, CH), CH)
            kseg = segment(c * CH + lax.broadcasted_iota(jnp.int32, (CH, 1), 0))
            same = kseg == qseg
            out = []
            for h in range(NH):
                s = dot(kv_ref[rows, HS * h : HS * (h + 1)], qt_ref[i, HS * h : HS * (h + 1), :])
                s = jnp.where(same, s, NEG)
                s_scr[h, rows, :] = s
                out.append(jnp.maximum(ms[h], jnp.max(s, axis=0, keepdims=True)))
            return tuple(out)

        ms = lax.fori_loop(c0, c1, pass1, tuple(jnp.full((1, BLK), NEG, jnp.float32) for _ in range(NH)))
        ot[...] = jnp.zeros_like(ot)
        gt[...] = jnp.zeros_like(gt)

        def pass2(c, ts):
            rows = pl.ds(pl.multiple_of(c * CH, CH), CH)
            out = []
            for h in range(NH):
                p = jnp.exp(s_scr[h, rows, :] - ms[h])
                out.append(ts[h] + jnp.sum(p, axis=0, keepdims=True))
                pb = p.astype(jnp.bfloat16)
                p_scr[h, rows, :] = pb
                ot[HS * h : HS * (h + 1), :] += dot(kvt[GW + HS * h : GW + HS * (h + 1), rows], pb)
            return tuple(out)

        ts = lax.fori_loop(c0, c1, pass2, tuple(jnp.zeros((1, BLK), jnp.float32) for _ in range(NH)))

        deltas, rts, qrs, urs = [], [], [], []
        for h in range(NH):
            cols = slice(HS * h, HS * (h + 1))
            rt = 1.0 / ts[h]
            o = (ot[cols, :] / ts[h]).astype(jnp.bfloat16)
            outt_ref[i, cols, :] = o
            u = ut_ref[i, cols, :].astype(jnp.float32)
            deltas.append(jnp.sum(u * o.astype(jnp.float32), axis=0, keepdims=True))
            rts.append(rt)
            qrs.append((qt_ref[i, cols, :].astype(jnp.float32) * rt).astype(jnp.bfloat16))
            urs.append((u * rt).astype(jnp.bfloat16))

        def pass3(c, carry):
            rows = pl.ds(pl.multiple_of(c * CH, CH), CH)
            kgs, vgs = [], []
            for h in range(NH):
                cols = slice(HS * h, HS * (h + 1))
                dp = dot(kv_ref[rows, GW + HS * h : GW + HS * (h + 1)], ut_ref[i, cols, :])
                pb = p_scr[h, rows, :]
                ds = (pb.astype(jnp.float32) * (dp - deltas[h])).astype(jnp.bfloat16)
                gt[cols, :] += dot(kvt[cols, rows], ds)
                kgs.append(dot_nt(ds, qrs[h]))
                vgs.append(dot_nt(pb, urs[h]))
            acc[rows, :] += jnp.concatenate(kgs + vgs, axis=1)
            return carry

        lax.fori_loop(c0, c1, pass3, 0)
        g = jnp.concatenate([gt[HS * h : HS * (h + 1), :] * (rts[h] * SCALE) for h in range(NH)], axis=0)
        qg_ref[i] = g.T.astype(jnp.bfloat16)

    kvg_ref[...] = acc[...].astype(jnp.bfloat16)


def attend(scalars, qt, ut, kv):
    bf = jnp.bfloat16
    return pl.pallas_call(
        attend_kernel,
        out_shape=(
            jax.ShapeDtypeStruct((4, GW, BLK), bf),
            jax.ShapeDtypeStruct((4, BLK, GW), bf),
            jax.ShapeDtypeStruct((8 * BLK, 2 * GW), bf),
        ),
        in_specs=[pl.BlockSpec(memory_space=pltpu.SMEM)] + [pl.BlockSpec(memory_space=VMEM)] * 3,
        out_specs=[pl.BlockSpec(memory_space=VMEM)] * 3,
        scratch_shapes=[
            VMEM((NH, 8 * BLK, BLK), jnp.float32),
            VMEM((NH, 8 * BLK, BLK), bf),
            VMEM((2 * GW, 8 * BLK), bf),
            VMEM((8 * BLK, 2 * GW), jnp.float32),
            VMEM((GW, BLK), jnp.float32),
            VMEM((GW, BLK), jnp.float32),
        ],
        compiler_params=pltpu.CompilerParams(vmem_limit_bytes=LIMIT),
        name="attend",
    )(scalars, qt, ut, kv)


def reduce_kernel(
    outt_ref, qg_ref, kvg_ref, nt_ref,
    out_ref, wg_ref,
    zland, oland, s1q, r1q, s1k, r1k, s2q, r2q, s2k, r2k, s3, r3,
    zs, zr, os, orr, cs, cr, qs, qr, ks, kr, xs, xr,
):
    x, y, zh, zl, core = coords()
    z = zh * 2 + zl
    zp = dev(x, y, 1 - zh, zl, core)
    cp = dev(x, y, zh, zl, 1 - core)
    xd = [dev(mod4(x + d), y, zh, zl, core) for d in (1, 2, 3)]
    offsets = [(a, b) for a in range(4) for b in range(4) if (a, b) != (0, 0)]

    def yz(a, b):
        yy, zz = mod4(y + a), mod4(z + b)
        return yy, zz // 2, lax.rem(zz, 2)

    yzd = []
    for a, b in offsets:
        yy, hh, ll = yz(a, b)
        yzd.append((dev(x, yy, hh, ll, core), (ll * 4 + yy) * 2 + hh))
    greet([cp] + xd + [d for d, _ in yzd])

    def rcopy(src, dst, ss, rs, to):
        return pltpu.make_async_remote_copy(
            src_ref=src, dst_ref=dst, send_sem=ss, recv_sem=rs, device_id=to, device_id_type=MESH
        )

    zc = rcopy(kvg_ref.at[1 - zh], zland, zs, zr, zp)
    zc.start()
    oc = []
    for i, d in enumerate((1, 2, 3)):
        c = rcopy(outt_ref.at[mod4(x + d)], oland.at[x], os.at[i], orr.at[i], xd[i])
        c.start()
        oc.append(c)
    oland[x] = outt_ref[x]

    def core_step(g, s1, r1, i):
        s1[...] = dot(nt_ref[1 - core], g).astype(jnp.bfloat16)
        c = rcopy(s1, r1, cs.at[i], cr.at[i], cp)
        c.start()
        return c, dot(nt_ref[core], g)

    def spread(c, mine, r1, s2, r2, ss, rs):
        c.wait()
        both = (mine + r1[...].astype(jnp.float32)).astype(jnp.bfloat16)
        for j in range(16):
            s2[j] = both[48 * j : 48 * (j + 1), :]
        copies = []
        for i, (to, j) in enumerate(yzd):
            c2 = rcopy(s2.at[j], r2.at[i], ss.at[i], rs.at[i], to)
            c2.start()
            copies.append(c2)
        return copies

    me = (zl * 4 + y) * 2 + zh
    cq, mine = core_step(qg_ref[...], s1q, r1q, 0)
    qc = spread(cq, mine, r1q, s2q, r2q, qs, qr)
    for c in oc:
        c.wait()
    for g in range(4):
        out_ref[:, GW * g : GW * (g + 1)] = oland[g].astype(jnp.float32).T.astype(jnp.bfloat16)
    zc.wait()
    g = (kvg_ref[zh].astype(jnp.float32) + zland[...].astype(jnp.float32)).astype(jnp.bfloat16)
    ck, mine = core_step(g, s1k, r1k, 1)
    kc = spread(ck, mine, r1k, s2k, r2k, ks, kr)

    def total(copies, s2, r2):
        t = s2[me].astype(jnp.float32)
        for i, c in enumerate(copies):
            c.wait()
            t = t + r2[i].astype(jnp.float32)
        return t

    tq = total(qc, s2q, r2q)
    tk = total(kc, s2k, r2k)
    for xb in range(4):
        s3[xb, 0:12, 0:GW] = tq[12 * xb : 12 * (xb + 1), :]
        s3[xb, 0:12, 256 : 256 + 2 * GW] = tk[12 * xb : 12 * (xb + 1), :]
    xc = []
    for i, d in enumerate((1, 2, 3)):
        c = rcopy(s3.at[mod4(x + d)], r3.at[x], xs.at[i], xr.at[i], xd[i])
        c.start()
        xc.append(c)
    r3[x] = s3[x]
    for c in xc:
        c.wait()
    for xb in range(4):
        wg_ref[:, GW * xb : GW * (xb + 1)] = r3[xb, 0:12, 0:GW]
        wg_ref[:, WIDTH + GW * xb : WIDTH + GW * (xb + 1)] = r3[xb, 0:12, 256 : 256 + GW]
        wg_ref[:, 2 * WIDTH + GW * xb : 2 * WIDTH + GW * (xb + 1)] = r3[xb, 0:12, 256 + GW : 256 + 2 * GW]


def reduce(outt, qg, kvg, nt):
    bf = jnp.bfloat16
    dma = pltpu.SemaphoreType.DMA
    return pl.pallas_call(
        reduce_kernel,
        out_shape=(
            jax.ShapeDtypeStruct((BLK, WIDTH), bf),
            jax.ShapeDtypeStruct((12, 3 * WIDTH), jnp.float32),
        ),
        in_specs=[pl.BlockSpec(memory_space=VMEM)] * 4,
        out_specs=[pl.BlockSpec(memory_space=VMEM)] * 2,
        scratch_shapes=[
            VMEM((4 * BLK, 2 * GW), bf),
            VMEM((4, GW, BLK), bf),
            VMEM((WIDTH, GW), bf),
            VMEM((WIDTH, GW), bf),
            VMEM((WIDTH, 2 * GW), bf),
            VMEM((WIDTH, 2 * GW), bf),
            VMEM((16, 48, GW), bf),
            VMEM((15, 48, GW), bf),
            VMEM((16, 48, 2 * GW), bf),
            VMEM((15, 48, 2 * GW), bf),
            VMEM((4, 16, 640), jnp.float32),
            VMEM((4, 16, 640), jnp.float32),
            dma, dma, dma((3,)), dma((3,)), dma((2,)), dma((2,)),
            dma((15,)), dma((15,)), dma((15,)), dma((15,)), dma((3,)), dma((3,)),
        ],
        compiler_params=pltpu.CompilerParams(collective_id=1, has_side_effects=True, vmem_limit_bytes=LIMIT),
        name="reduce",
    )(outt, qg, kvg, nt)


def shards(hidden, masked, clip_lengths, qkv_weight, cotangent):
    lengths = clip_lengths[0]
    e0 = lengths[0]
    scalars = jnp.stack([e0, e0 + lengths[1], (lax.axis_index("seq") // 4) * (4 * BLK)])
    qt, ut, kv, nt = project(hidden, masked[:, None], cotangent, qkv_weight)
    outt, qg, kvg = attend(scalars, qt, ut, kv.reshape(8 * BLK, 2 * GW))
    out, wg = reduce(outt, qg.reshape(4 * BLK, GW), kvg.reshape(2, 4 * BLK, 2 * GW), nt)
    return out, wg


def solution(mesh):
    in_specs = (
        P(("dp", "seq"), None),
        P(("dp", "seq")),
        P("dp", None),
        P(),
        P(("dp", "seq"), None),
    )
    out_specs = (P(("dp", "seq"), None), P(("dp", "seq"), None))
    return jax.shard_map(shards, mesh=mesh, in_specs=in_specs, out_specs=out_specs, check_vma=False)
```

```python
import functools

import jax
import jax.numpy as jnp
from jax import lax
from jax.experimental import pallas as pl
from jax.experimental.pallas import tpu as pltpu
from jax.sharding import PartitionSpec as P

MESH = pl.DeviceIdType.MESH
VMEM = pltpu.VMEM
BF = jnp.bfloat16
F32 = jnp.float32
HS = 64
NH = 3
GW = NH * HS
BLK = 256
HALF = 4 * BLK
D = 1536
WIDTH = 768
NEG = -1e30
SCALE = 0.125
LIMIT = 62 * 1024 * 1024
STEPS = (1, 2, 3)


def mod4(v):
    return lax.rem(v, 4)


def dot(a, b):
    return jnp.dot(a, b, preferred_element_type=F32)


def dot_nt(a, b):
    return lax.dot_general(a, b, (((1,), (1,)), ((), ())), preferred_element_type=F32)


def lanes(at, size):
    return pl.ds(pl.multiple_of(at, size), size)


def main_kernel(
    len_ref, hidden_ref, mask_ref, cot_ref, w_ref,
    oland, r3,
    land, wbuf, usend, ut, kv, kvt, qz, uz, nt, s_scr, d_scr, p_scr, g_scr,
    qg, own, zsend, zland, osend, s1, r1, mine, s2, r2, s4, r4, s3,
    wsem, hs, hr, ks, kr, us, ur, zs, zr, osm, orm, cs, cr, ys, yr, vs, vr, xs, xr,
):
    dp = lax.axis_index("dp")
    sq = lax.axis_index("seq")
    core, y, zl = lax.rem(dp, 2), lax.rem(dp // 2, 4), dp // 8
    x, zh = lax.rem(sq, 4), sq // 4
    z = zh * 2 + zl

    def dev(x, y, z, core):
        return ((lax.rem(z, 2) * 4 + y) * 2 + core, (z // 2) * 4 + x)

    xd = [dev(mod4(x + d), y, z, core) for d in STEPS]
    yd = [dev(x, mod4(y + d), z, core) for d in STEPS]
    zd = [dev(x, y, mod4(z + d), core) for d in STEPS]
    cp = dev(x, y, z, 1 - core)
    zp = zd[1]
    right, far, left = xd
    lane0 = (3 * x) // 2 * 128
    odd = lax.rem(x, 2) == 1

    def rcopy(src, dst, ss, rs, to):
        return pltpu.make_async_remote_copy(
            src_ref=src, dst_ref=dst, send_sem=ss, recv_sem=rs, device_id=to, device_id_type=MESH
        )

    wcopies = []
    for j in range(3):
        c = pltpu.make_async_copy(
            w_ref.at[:, pl.ds(pl.multiple_of(WIDTH * j + lane0, 128), 256)], wbuf.at[j], wsem.at[j]
        )
        c.start()
        wcopies.append(c)

    barrier = pltpu.get_barrier_semaphore()
    partners = [cp] + xd + yd + zd
    for p in partners:
        pl.semaphore_signal(barrier, inc=1, device_id=p, device_id_type=MESH)
    pl.semaphore_wait(barrier, len(partners))

    half = BLK // 2
    top, bot = pl.ds(0, half), pl.ds(half, half)
    a0 = rcopy(hidden_ref.at[top], land.at[0, top], hs.at[0], hr.at[0], right)
    a1 = rcopy(hidden_ref.at[bot], land.at[1, bot], hs.at[1], hr.at[1], left)
    a2 = rcopy(hidden_ref.at[bot], land.at[0, bot], hs.at[2], hr.at[2], right)
    a3 = rcopy(hidden_ref.at[top], land.at[1, top], hs.at[3], hr.at[3], left)
    for c in (a0, a1, a2, a3):
        c.start()
    b0 = rcopy(land.at[0, top], land.at[2, top], hs.at[4], hr.at[4], right)
    b1 = rcopy(land.at[1, bot], land.at[2, bot], hs.at[5], hr.at[5], left)

    qz[...] = jnp.zeros_like(qz)
    uz[...] = jnp.zeros_like(uz)
    keep = mask_ref[...] == 1
    for g in range(4):
        u = cot_ref[:, GW * g : GW * (g + 1)].astype(F32).T
        usend[g] = jnp.where(keep, u, 0.0).astype(BF)
    for c in wcopies:
        c.wait()

    def slot(xb):
        return jnp.where(zh == 0, xb, 3 - xb)

    def pick(r):
        return jnp.where(odd, r[:, 64:256], r[:, 0:192])

    def turn(c):
        t = jnp.where(zh == 0, c, 7 - c)
        for h in range(NH):
            kvt[h, :, lanes(t * BLK, BLK)] = kv[c, h].T

    def kvcopy(c, xb):
        return rcopy(kv.at[c], kv.at[c], ks.at[xb], kr.at[xb], zp)

    def process(h, xb):
        h = h.astype(F32)
        scale = lax.rsqrt(jnp.mean(h * h, axis=1, keepdims=True) + 1e-06)
        normed = (h * scale).astype(BF)
        k = pick(dot(normed, wbuf[1]))
        v = pick(dot(normed, wbuf[2]))
        c = zh * 4 + xb
        for i in range(NH):
            cols = slice(HS * i, HS * (i + 1))
            kv[c, i] = jnp.concatenate([k[:, cols], v[:, cols]], axis=1).astype(BF)
        kvcopy(c, xb).start()
        q = (pick(dot(normed, wbuf[0])).astype(BF).astype(F32) * SCALE).T.astype(BF)
        for i in range(NH):
            qz[i, 0:HS, lanes(slot(xb) * BLK, BLK)] = q[HS * i : HS * (i + 1), :]
        turned = normed.T
        for j in range(8):
            for par in range(2):
                at = 192 * j + 96 * par
                nt[par, 96 * j : 96 * (j + 1), lanes(xb * BLK, BLK)] = turned[at : at + 96, :]
        turn(c)

    process(hidden_ref[...], x)
    a0.wait_recv()
    b0.start()
    a1.wait_recv()
    b1.start()
    a2.wait_recv()
    process(land[0], mod4(x + 3))
    a3.wait_recv()
    process(land[1], mod4(x + 1))
    for c in (a0, a1, a2, a3, b0, b1):
        c.wait_send()
    ucopies = []
    for i, d in enumerate(STEPS):
        c = rcopy(usend.at[mod4(x + d)], ut.at[x], us.at[i], ur.at[i], xd[i])
        c.start()
        ucopies.append(c)
    ut[x] = usend[x]
    b0.wait_recv()
    b1.wait_recv()
    process(land[2], mod4(x + 2))
    for xb in range(4):
        theirs = (1 - zh) * 4 + xb
        kvcopy(zh * 4 + xb, xb).wait_send()
        kvcopy(theirs, xb).wait_recv()
        turn(theirs)

    def zcopy(h):
        return rcopy(zsend.at[h], zland.at[h], zs.at[h], zr.at[h], zp)

    def ccopy(h):
        return rcopy(s1.at[h], r1.at[h], cs.at[h], cr.at[h], cp)

    def ycopy(h, i):
        return rcopy(s2.at[h, mod4(y + STEPS[i])], r2.at[h, i], ys.at[h, i], yr.at[h, i], yd[i])

    def vcopy(h, i):
        return rcopy(s4.at[h, mod4(z + STEPS[i])], r4.at[h, i], vs.at[h, i], vr.at[h, i], zd[i])

    def ocopy(h, i):
        rows = pl.ds(pl.multiple_of(h * HS, HS), HS)
        return rcopy(osend.at[h, mod4(x + STEPS[i])], oland.at[x, rows], osm.at[h, i], orm.at[h, i], xd[i])

    def to_core(h):
        zcopy(h).wait()
        g = jnp.concatenate([qg[h], (own[h] + zland[h].astype(F32)).astype(BF)], axis=0)
        s1[h] = dot_nt(nt[1 - core], g).astype(BF)
        ccopy(h).start()
        mine[...] = dot_nt(nt[core], g)

    def to_y(h):
        ccopy(h).wait()
        both = (mine[...] + r1[h].astype(F32)).astype(BF)
        for l in range(2):
            for yy in range(4):
                for u in range(2):
                    row = 384 * l + 96 * yy + 48 * u
                    s2[h, yy, 2 * u + l] = both[row : row + 48, :]
        for i in range(3):
            ycopy(h, i).start()

    def to_z(h):
        t = s2[h, y].astype(F32)
        for i in range(3):
            ycopy(h, i).wait()
            t = t + r2[h, i].astype(F32)
        s4[h] = t.astype(BF)
        for i in range(3):
            vcopy(h, i).start()

    e0 = len_ref[0, 0]
    e1 = e0 + len_ref[0, 1]

    def segment(pos):
        return (pos >= e0).astype(jnp.int32) + (pos >= e1).astype(jnp.int32)

    def key_block(t):
        return jnp.where(zh == 0, t, 7 - t)

    def slots(t):
        return range(max(0, t - 4), 4)

    def qpos(j):
        return zh * HALF + BLK * jnp.where(zh == 0, j, 3 - j)

    qsegs = [segment(qpos(j) + lax.broadcasted_iota(jnp.int32, (1, BLK), 1)) for j in range(4)]

    def at(j):
        return slice(BLK * j, BLK * (j + 1))

    def head(h, carry):
        ms = [jnp.full((1, BLK), NEG, F32) for _ in range(4)]
        for t in range(8):
            c = key_block(t)
            kseg = segment(c * BLK + lax.broadcasted_iota(jnp.int32, (BLK, 1), 0))
            for j in slots(t):
                s = dot(kv[c, h], qz[h, :, at(j)])
                s = jnp.where(kseg == qsegs[j], s, NEG)
                s_scr[at(t), at(j)] = s
                ms[j] = jnp.maximum(ms[j], jnp.max(s, axis=0, keepdims=True))

        @pl.when(h == 0)
        def _():
            for c in ucopies:
                c.wait()
            for xb in range(4):
                for i in range(NH):
                    uz[i, HS : 2 * HS, lanes(slot(xb) * BLK, BLK)] = ut[xb, HS * i : HS * (i + 1), :]

        @pl.when(h > 0)
        def _():
            to_core(h - 1)

        ts = [jnp.zeros((1, BLK), F32) for _ in range(4)]
        for t in range(8):
            c = key_block(t)
            for j in slots(t):
                p = jnp.exp(s_scr[at(t), at(j)] - ms[j])
                ts[j] = ts[j] + jnp.sum(p, axis=0, keepdims=True)
                p_scr[at(t), at(j)] = p.astype(BF)
                d_scr[at(t), at(j)] = dot(kv[c, h], uz[h, :, at(j)])

        @pl.when(h > 0)
        def _():
            to_y(h - 1)

        rts, deltas, qrs, urs = [], [], [], []
        for j in range(4):
            rows = slice(0, BLK * (5 + j))
            o = (dot(kvt[h, HS : 2 * HS, rows], p_scr[rows, at(j)]) / ts[j]).astype(BF)
            osend[h, jnp.where(zh == 0, j, 3 - j)] = o
            u = uz[h, HS : 2 * HS, at(j)].astype(F32)
            rt = 1.0 / ts[j]
            rts.append(rt)
            deltas.append(jnp.sum(u * o.astype(F32), axis=0, keepdims=True))
            qrs.append((qz[h, 0:HS, at(j)].astype(F32) * rt).astype(BF))
            urs.append((u * rt).astype(BF))
        for i in range(3):
            ocopy(h, i).start()
        oland[x, pl.ds(pl.multiple_of(h * HS, HS), HS), :] = osend[h, x]

        for t in (7, 6, 5, 4, 3, 2, 1, 0):
            kg = jnp.zeros((HS, BLK), F32)
            vg = jnp.zeros((HS, BLK), F32)
            for j in slots(t):
                pb = p_scr[at(t), at(j)]
                ds = (pb.astype(F32) * (d_scr[at(t), at(j)] - deltas[j])).astype(BF)
                g_scr[at(t), at(j)] = ds
                kg = kg + dot_nt(qrs[j], ds)
                vg = vg + dot_nt(urs[j], pb)
            both = jnp.concatenate([kg, vg], axis=0)
            if t >= 4:
                zsend[h, :, lanes(jnp.where(zh == 0, t - 4, 7 - t) * BLK, BLK)] = both.astype(BF)
            else:
                own[h, :, lanes(jnp.where(zh == 0, t, 3 - t) * BLK, BLK)] = both
            if t == 4:
                zcopy(h).start()
        for j in range(4):
            rows = slice(0, BLK * (5 + j))
            g = dot(kvt[h, 0:HS, rows], g_scr[rows, at(j)]) * (rts[j] * SCALE)
            qg[h, :, lanes(jnp.where(zh == 0, j, 3 - j) * BLK, BLK)] = g.astype(BF)

        @pl.when(h > 0)
        def _():
            to_z(h - 1)

        return carry

    lax.fori_loop(0, NH, head, 0)
    to_core(NH - 1)
    to_y(NH - 1)
    to_z(NH - 1)

    for h in range(NH):
        t = s4[h, z].astype(F32)
        for i in range(3):
            vcopy(h, i).wait()
            t = t + r4[h, i].astype(F32)
        for xb in range(4):
            s3[xb, 0:12, GW * h : GW * (h + 1)] = t[12 * xb : 12 * (xb + 1), :]
    xc = []
    for i, d in enumerate(STEPS):
        c = rcopy(s3.at[mod4(x + d)], r3.at[x], xs.at[i], xr.at[i], xd[i])
        c.start()
        xc.append(c)
    r3[x] = s3[x]
    for h in range(NH):
        for i in range(3):
            ocopy(h, i).wait()
    for c in xc:
        c.wait()


def main(lengths, hidden, mask, cot, w):
    dma = pltpu.SemaphoreType.DMA
    return pl.pallas_call(
        main_kernel,
        out_shape=(
            jax.ShapeDtypeStruct((4, GW, BLK), BF),
            jax.ShapeDtypeStruct((4, 16, 640), F32),
        ),
        in_specs=[pl.BlockSpec(memory_space=pltpu.SMEM)]
        + [pl.BlockSpec(memory_space=VMEM)] * 3
        + [pl.BlockSpec(memory_space=pl.ANY)],
        out_specs=[pl.BlockSpec(memory_space=VMEM)] * 2,
        scratch_shapes=[
            VMEM((3, BLK, D), BF),
            VMEM((3, D, 256), BF),
            VMEM((4, GW, BLK), BF),
            VMEM((4, GW, BLK), BF),
            VMEM((8, NH, BLK, 2 * HS), BF),
            VMEM((NH, 2 * HS, 8 * BLK), BF),
            VMEM((NH, 2 * HS, HALF), BF),
            VMEM((NH, 2 * HS, HALF), BF),
            VMEM((2, WIDTH, HALF), BF),
            VMEM((8 * BLK, HALF), F32),
            VMEM((8 * BLK, HALF), F32),
            VMEM((8 * BLK, HALF), BF),
            VMEM((8 * BLK, HALF), BF),
            VMEM((NH, HS, HALF), BF),
            VMEM((NH, 2 * HS, HALF), F32),
            VMEM((NH, 2 * HS, HALF), BF),
            VMEM((NH, 2 * HS, HALF), BF),
            VMEM((NH, 4, HS, BLK), BF),
            VMEM((NH, WIDTH, GW), BF),
            VMEM((NH, WIDTH, GW), BF),
            VMEM((WIDTH, GW), F32),
            VMEM((NH, 4, 4, 48, GW), BF),
            VMEM((NH, 3, 4, 48, GW), BF),
            VMEM((NH, 4, 48, GW), BF),
            VMEM((NH, 3, 48, GW), BF),
            VMEM((4, 16, 640), F32),
            dma((3,)), dma((6,)), dma((6,)), dma((4,)), dma((4,)), dma((3,)), dma((3,)),
            dma((NH,)), dma((NH,)), dma((NH, 3)), dma((NH, 3)), dma((NH,)), dma((NH,)),
            dma((NH, 3)), dma((NH, 3)), dma((NH, 3)), dma((NH, 3)), dma((3,)), dma((3,)),
        ],
        compiler_params=pltpu.CompilerParams(collective_id=0, has_side_effects=True, vmem_limit_bytes=LIMIT),
        name="main",
    )(lengths, hidden, mask, cot, w)


def lay_out_kernel(ot_ref, w_ref, out_ref, wg_ref):
    for g in range(4):
        at = GW * g
        out_ref[:, at : at + GW] = ot_ref[g].astype(F32).T.astype(BF)
        for h in range(NH):
            for part in range(3):
                src = GW * h + HS * part
                to = WIDTH * part + at + HS * h
                wg_ref[:, to : to + HS] = w_ref[g, 0:12, src : src + HS]


def lay_out(ot, w):
    return pl.pallas_call(
        lay_out_kernel,
        out_shape=(
            jax.ShapeDtypeStruct((BLK, WIDTH), BF),
            jax.ShapeDtypeStruct((12, 3 * WIDTH), F32),
        ),
        in_specs=[pl.BlockSpec(memory_space=VMEM)] * 2,
        out_specs=[pl.BlockSpec(memory_space=VMEM)] * 2,
        name="lay_out",
    )(ot, w)


def shards(hidden, masked, clip_lengths, qkv_weight, cotangent):
    ot, w = main(clip_lengths, hidden, masked.reshape(1, BLK), cotangent, qkv_weight)
    return lay_out(ot, w)


def solution(mesh):
    in_specs = (
        P(("dp", "seq"), None),
        P(("dp", "seq")),
        P("dp", None),
        P(),
        P(("dp", "seq"), None),
    )
    out_specs = (P(("dp", "seq"), None), P(("dp", "seq"), None))
    return jax.shard_map(shards, mesh=mesh, in_specs=in_specs, out_specs=out_specs, check_vma=False)
```

```python
import functools

import jax
import jax.numpy as jnp
from jax import lax
from jax.experimental import pallas as pl
from jax.experimental.pallas import tpu as pltpu
from jax.sharding import PartitionSpec as P

MESH = pl.DeviceIdType.MESH
VMEM = pltpu.VMEM
BF = jnp.bfloat16
F32 = jnp.float32
HS = 64
NH = 3
GW = NH * HS
BLK = 256
HALF = 4 * BLK
D = 1536
WIDTH = 768
NEG = -1e30
SCALE = 0.125
LIMIT = 62 * 1024 * 1024
STEPS = (1, 2, 3)


def mod4(v):
    return lax.rem(v, 4)


def dot(a, b):
    return jnp.dot(a, b, preferred_element_type=F32)


def dot_nt(a, b):
    return lax.dot_general(a, b, (((1,), (1,)), ((), ())), preferred_element_type=F32)


def lanes(at, size):
    return pl.ds(pl.multiple_of(at, size), size)


def main_kernel(
    len_ref, hidden_ref, mask_ref, cot_ref, w_ref,
    oland, r3,
    land, wbuf, usend, ut, kv, kvt, qz, uz, nt, s_scr, d_scr, p_scr, g_scr,
    qg, own, zsend, zland, osend, s1, r1, mine, s2, r2, s4, r4, s5, r5, s3, nbuf, mx,
    wsem, hs, hr, ks, kr, us, ur, zs, zr, osm, orm, cs, cr, ys, yr, vs, vr, ds, dr, xs, xr,
):
    dp = lax.axis_index("dp")
    sq = lax.axis_index("seq")
    core, y, zl = lax.rem(dp, 2), lax.rem(dp // 2, 4), dp // 8
    x, zh = lax.rem(sq, 4), sq // 4
    z = zh * 2 + zl

    def dev(x, y, z, core):
        return ((lax.rem(z, 2) * 4 + y) * 2 + core, (z // 2) * 4 + x)

    xd = [dev(mod4(x + d), y, z, core) for d in STEPS]
    yd = [dev(x, mod4(y + d), z, core) for d in STEPS]
    zd = [dev(x, y, mod4(z + d), core) for d in STEPS]
    cp = dev(x, y, z, 1 - core)
    yzd = []
    for a in range(4):
        for b in range(4):
            if (a, b) != (0, 0):
                yy, zz = mod4(y + a), mod4(z + b)
                yzd.append((dev(x, yy, zz, core), yy * 4 + zz))
    zp = zd[1]
    right, far, left = xd
    lane0 = (3 * x) // 2 * 128
    odd = lax.rem(x, 2) == 1

    def rcopy(src, dst, ss, rs, to):
        return pltpu.make_async_remote_copy(
            src_ref=src, dst_ref=dst, send_sem=ss, recv_sem=rs, device_id=to, device_id_type=MESH
        )

    wcopies = []
    for j in range(3):
        c = pltpu.make_async_copy(
            w_ref.at[:, pl.ds(pl.multiple_of(WIDTH * j + lane0, 128), 256)], wbuf.at[j], wsem.at[j]
        )
        c.start()
        wcopies.append(c)

    barrier = pltpu.get_barrier_semaphore()
    partners = [cp] + xd + [to for to, _ in yzd]
    for p in partners:
        pl.semaphore_signal(barrier, inc=1, device_id=p, device_id_type=MESH)
    pl.semaphore_wait(barrier, len(partners))

    half = BLK // 2
    top, bot = pl.ds(0, half), pl.ds(half, half)
    a0 = rcopy(hidden_ref.at[top], land.at[0, top], hs.at[0], hr.at[0], right)
    a1 = rcopy(hidden_ref.at[bot], land.at[1, bot], hs.at[1], hr.at[1], left)
    a2 = rcopy(hidden_ref.at[bot], land.at[0, bot], hs.at[2], hr.at[2], right)
    a3 = rcopy(hidden_ref.at[top], land.at[1, top], hs.at[3], hr.at[3], left)
    for c in (a0, a1, a2, a3):
        c.start()
    b0 = rcopy(land.at[0, top], land.at[2, top], hs.at[4], hr.at[4], right)
    b1 = rcopy(land.at[1, bot], land.at[2, bot], hs.at[5], hr.at[5], left)

    qz[...] = jnp.zeros_like(qz)
    uz[...] = jnp.zeros_like(uz)
    keep = mask_ref[...] == 1
    for g in range(4):
        u = cot_ref[:, GW * g : GW * (g + 1)].astype(F32).T
        usend[g] = jnp.where(keep, u, 0.0).astype(BF)
    for c in wcopies:
        c.wait()

    def slot(xb):
        return jnp.where(zh == 0, xb, 3 - xb)

    def pick(r):
        return jnp.where(odd, r[:, 64:256], r[:, 0:192])

    def turn(c):
        t = jnp.where(zh == 0, c, 7 - c)
        for h in range(NH):
            kvt[h, :, lanes(t * BLK, BLK)] = kv[c, h].T

    def kvcopy(c, xb):
        return rcopy(kv.at[c], kv.at[c], ks.at[xb], kr.at[xb], zp)

    def process(h, xb):
        h = h.astype(F32)
        scale = lax.rsqrt(jnp.mean(h * h, axis=1, keepdims=True) + 1e-06)
        normed = (h * scale).astype(BF)
        nbuf[...] = normed
        k = pick(dot(normed, wbuf[1]))
        v = pick(dot(normed, wbuf[2]))
        c = zh * 4 + xb
        for i in range(NH):
            cols = slice(HS * i, HS * (i + 1))
            kv[c, i] = jnp.concatenate([k[:, cols], v[:, cols]], axis=1).astype(BF)
        kvcopy(c, xb).start()

    def finish(xb):
        normed = nbuf[...]
        q = (pick(dot(normed, wbuf[0])).astype(BF).astype(F32) * SCALE).T.astype(BF)
        for i in range(NH):
            qz[i, 0:HS, lanes(slot(xb) * BLK, BLK)] = q[HS * i : HS * (i + 1), :]
        turned = normed.T
        for j in range(8):
            for par in range(2):
                at = 192 * j + 96 * par
                nt[par, 96 * j : 96 * (j + 1), lanes(xb * BLK, BLK)] = turned[at : at + 96, :]
        turn(zh * 4 + xb)

    def arrive(xb):
        theirs = (1 - zh) * 4 + xb
        kvcopy(theirs, xb).wait_recv()
        turn(theirs)

    process(hidden_ref[...], x)
    a0.wait_recv()
    b0.start()
    a1.wait_recv()
    b1.start()
    finish(x)
    a2.wait_recv()
    process(land[0], mod4(x + 3))
    finish(mod4(x + 3))
    a3.wait_recv()
    process(land[1], mod4(x + 1))
    finish(mod4(x + 1))
    arrive(x)
    for c in (a0, a1, a2, a3, b0, b1):
        c.wait_send()
    ucopies = []
    for i, d in enumerate(STEPS):
        c = rcopy(usend.at[mod4(x + d)], ut.at[x], us.at[i], ur.at[i], xd[i])
        c.start()
        ucopies.append(c)
    ut[x] = usend[x]
    b0.wait_recv()
    b1.wait_recv()
    process(land[2], mod4(x + 2))
    finish(mod4(x + 2))

    def zcopy(h, part):
        return rcopy(zsend.at[h, part], zland.at[h, part], zs.at[h, part], zr.at[h, part], zp)

    def ccopy(h):
        return rcopy(s1.at[h], r1.at[h], cs.at[h], cr.at[h], cp)

    def ycopy(h, i):
        return rcopy(s2.at[h, mod4(y + STEPS[i])], r2.at[h, i], ys.at[h, i], yr.at[h, i], yd[i])

    def vcopy(h, i):
        return rcopy(s4.at[h, mod4(z + STEPS[i])], r4.at[h, i], vs.at[h, i], vr.at[h, i], zd[i])

    def ocopy(h, i):
        rows = pl.ds(pl.multiple_of(h * HS, HS), HS)
        return rcopy(osend.at[h, mod4(x + STEPS[i])], oland.at[x, rows], osm.at[h, i], orm.at[h, i], xd[i])

    def to_core(h):
        parts = [qg[h]]
        for part in range(2):
            zcopy(h, part).wait()
            parts.append((own[h, part] + zland[h, part].astype(F32)).astype(BF))
        g = jnp.concatenate(parts, axis=0)
        s1[h] = dot_nt(nt[1 - core], g).astype(BF)
        ccopy(h).start()
        mine[...] = dot_nt(nt[core], g)

    def to_y(h):
        ccopy(h).wait()
        both = (mine[...] + r1[h].astype(F32)).astype(BF)
        for l in range(2):
            for yy in range(4):
                for u in range(2):
                    row = 384 * l + 96 * yy + 48 * u
                    s2[h, yy, 2 * u + l] = both[row : row + 48, :]
        for i in range(3):
            ycopy(h, i).start()

    def to_z(h):
        t = s2[h, y].astype(F32)
        for i in range(3):
            ycopy(h, i).wait()
            t = t + r2[h, i].astype(F32)
        s4[h] = t.astype(BF)
        for i in range(3):
            vcopy(h, i).start()

    def dcopy(i):
        to, place = yzd[i]
        return rcopy(s5.at[place], r5.at[i], ds.at[i], dr.at[i], to)

    def to_yz(h):
        ccopy(h).wait()
        both = (mine[...] + r1[h].astype(F32)).astype(BF)
        for l in range(2):
            for yy in range(4):
                for u in range(2):
                    row = 384 * l + 96 * yy + 48 * u
                    s5[yy * 4 + 2 * u + l] = both[row : row + 48, :]
        for i in range(15):
            dcopy(i).start()

    e0 = len_ref[0, 0]
    e1 = e0 + len_ref[0, 1]

    def segment(pos):
        return (pos >= e0).astype(jnp.int32) + (pos >= e1).astype(jnp.int32)

    def key_block(t):
        return jnp.where(zh == 0, t, 7 - t)

    def slots(t):
        return range(max(0, t - 4), 4)

    def qpos(j):
        return zh * HALF + BLK * jnp.where(zh == 0, j, 3 - j)

    qsegs = [segment(qpos(j) + lax.broadcasted_iota(jnp.int32, (1, BLK), 1)) for j in range(4)]

    def at(j):
        return slice(BLK * j, BLK * (j + 1))

    def scores(h, steps):
        for t in steps:
            c = key_block(t)
            kseg = segment(c * BLK + lax.broadcasted_iota(jnp.int32, (BLK, 1), 0))
            for j in slots(t):
                s = dot(kv[c, h], qz[h, :, at(j)])
                s = jnp.where(kseg == qsegs[j], s, NEG)
                s_scr[at(t), at(j)] = s
                m = jnp.max(s, axis=0, keepdims=True)
                mx[0:1, at(j)] = m if t == 0 else jnp.maximum(mx[0:1, at(j)], m)

    def head(h, carry):
        scores(h, range(4, 8))

        @pl.when(h == 0)
        def _():
            for c in ucopies:
                c.wait()
            for xb in range(4):
                for i in range(NH):
                    uz[i, HS : 2 * HS, lanes(slot(xb) * BLK, BLK)] = ut[xb, HS * i : HS * (i + 1), :]

        ms = [mx[0:1, at(j)] for j in range(4)]
        ts = [jnp.zeros((1, BLK), F32) for _ in range(4)]
        for t in range(8):
            c = key_block(t)
            for j in slots(t):
                p = jnp.exp(s_scr[at(t), at(j)] - ms[j])
                ts[j] = ts[j] + jnp.sum(p, axis=0, keepdims=True)
                p_scr[at(t), at(j)] = p.astype(BF)
                d_scr[at(t), at(j)] = dot(kv[c, h], uz[h, :, at(j)])

        rts = [1.0 / ts[j] for j in range(4)]
        us_ = [uz[h, HS : 2 * HS, at(j)].astype(F32) for j in range(4)]
        urs = [(us_[j] * rts[j]).astype(BF) for j in range(4)]
        qrs = [(qz[h, 0:HS, at(j)].astype(F32) * rts[j]).astype(BF) for j in range(4)]

        def put(t, part, g):
            if t >= 4:
                zsend[h, part, :, lanes(jnp.where(zh == 0, t - 4, 7 - t) * BLK, BLK)] = g.astype(BF)
            else:
                own[h, part, :, lanes(jnp.where(zh == 0, t, 3 - t) * BLK, BLK)] = g

        def value_grad(t):
            g = jnp.zeros((HS, BLK), F32)
            for j in slots(t):
                g = g + dot_nt(urs[j], p_scr[at(t), at(j)])
            put(t, 1, g)

        def key_grad(t):
            g = jnp.zeros((HS, BLK), F32)
            for j in slots(t):
                ds_ = p_scr[at(t), at(j)].astype(F32) * (d_scr[at(t), at(j)] - deltas[j])
                ds_ = ds_.astype(BF)
                g_scr[at(t), at(j)] = ds_
                g = g + dot_nt(qrs[j], ds_)
            put(t, 0, g)

        for t in (7, 6, 5, 4):
            value_grad(t)
        zcopy(h, 1).start()

        deltas = []
        for j in range(4):
            rows = slice(0, BLK * (5 + j))
            o = (dot(kvt[h, HS : 2 * HS, rows], p_scr[rows, at(j)]) / ts[j]).astype(BF)
            osend[h, jnp.where(zh == 0, j, 3 - j)] = o
            deltas.append(jnp.sum(us_[j] * o.astype(F32), axis=0, keepdims=True))
        for i in range(3):
            ocopy(h, i).start()
        oland[x, pl.ds(pl.multiple_of(h * HS, HS), HS), :] = osend[h, x]

        for t in (7, 6, 5, 4):
            key_grad(t)
        zcopy(h, 0).start()

        @pl.when(h == 2)
        def _():
            to_z(0)

        @pl.when(h > 0)
        def _():
            to_core(h - 1)

        for t in (3, 2, 1, 0):
            value_grad(t)
            key_grad(t)
        for j in range(4):
            rows = slice(0, BLK * (5 + j))
            g = dot(kvt[h, 0:HS, rows], g_scr[rows, at(j)]) * (rts[j] * SCALE)
            qg[h, :, lanes(jnp.where(zh == 0, j, 3 - j) * BLK, BLK)] = g.astype(BF)

        @pl.when(h > 0)
        def _():
            to_y(h - 1)

        @pl.when(h < NH - 1)
        def _():
            scores(h + 1, range(4))

        return carry

    scores(0, range(4))
    for d in (3, 1, 2):
        arrive(mod4(x + d))
    for xb in range(4):
        kvcopy(zh * 4 + xb, xb).wait_send()
    lax.fori_loop(0, NH, head, 0)
    to_core(NH - 1)
    to_z(1)
    to_yz(NH - 1)

    for h in range(NH):
        if h < NH - 1:
            t = s4[h, z].astype(F32)
            for i in range(3):
                vcopy(h, i).wait()
                t = t + r4[h, i].astype(F32)
        else:
            t = s5[y * 4 + z].astype(F32)
            for i in range(15):
                dcopy(i).wait()
                t = t + r5[i].astype(F32)
        for xb in range(4):
            s3[xb, 0:12, GW * h : GW * (h + 1)] = t[12 * xb : 12 * (xb + 1), :]
    xc = []
    for i, d in enumerate(STEPS):
        c = rcopy(s3.at[mod4(x + d)], r3.at[x], xs.at[i], xr.at[i], xd[i])
        c.start()
        xc.append(c)
    r3[x] = s3[x]
    for h in range(NH):
        for i in range(3):
            ocopy(h, i).wait()
    for c in xc:
        c.wait()


def main(lengths, hidden, mask, cot, w):
    dma = pltpu.SemaphoreType.DMA
    return pl.pallas_call(
        main_kernel,
        out_shape=(
            jax.ShapeDtypeStruct((4, GW, BLK), BF),
            jax.ShapeDtypeStruct((4, 16, 640), F32),
        ),
        in_specs=[pl.BlockSpec(memory_space=pltpu.SMEM)]
        + [pl.BlockSpec(memory_space=VMEM)] * 3
        + [pl.BlockSpec(memory_space=pl.ANY)],
        out_specs=[pl.BlockSpec(memory_space=VMEM)] * 2,
        scratch_shapes=[
            VMEM((3, BLK, D), BF),
            VMEM((3, D, 256), BF),
            VMEM((4, GW, BLK), BF),
            VMEM((4, GW, BLK), BF),
            VMEM((8, NH, BLK, 2 * HS), BF),
            VMEM((NH, 2 * HS, 8 * BLK), BF),
            VMEM((NH, 2 * HS, HALF), BF),
            VMEM((NH, 2 * HS, HALF), BF),
            VMEM((2, WIDTH, HALF), BF),
            VMEM((8 * BLK, HALF), F32),
            VMEM((8 * BLK, HALF), F32),
            VMEM((8 * BLK, HALF), BF),
            VMEM((8 * BLK, HALF), BF),
            VMEM((NH, HS, HALF), BF),
            VMEM((NH, 2, HS, HALF), F32),
            VMEM((NH, 2, HS, HALF), BF),
            VMEM((NH, 2, HS, HALF), BF),
            VMEM((NH, 4, HS, BLK), BF),
            VMEM((NH, WIDTH, GW), BF),
            VMEM((NH, WIDTH, GW), BF),
            VMEM((WIDTH, GW), F32),
            VMEM((NH - 1, 4, 4, 48, GW), BF),
            VMEM((NH - 1, 3, 4, 48, GW), BF),
            VMEM((NH - 1, 4, 48, GW), BF),
            VMEM((NH - 1, 3, 48, GW), BF),
            VMEM((16, 48, GW), BF),
            VMEM((15, 48, GW), BF),
            VMEM((4, 16, 640), F32),
            VMEM((BLK, D), BF),
            VMEM((8, HALF), F32),
            dma((3,)), dma((6,)), dma((6,)), dma((4,)), dma((4,)), dma((3,)), dma((3,)),
            dma((NH, 2)), dma((NH, 2)), dma((NH, 3)), dma((NH, 3)), dma((NH,)), dma((NH,)),
            dma((NH - 1, 3)), dma((NH - 1, 3)), dma((NH - 1, 3)), dma((NH - 1, 3)), dma((15,)), dma((15,)),
            dma((3,)), dma((3,)),
        ],
        compiler_params=pltpu.CompilerParams(collective_id=0, has_side_effects=True, vmem_limit_bytes=LIMIT),
        name="main",
    )(lengths, hidden, mask, cot, w)


def lay_out_kernel(ot_ref, w_ref, out_ref, wg_ref):
    for g in range(4):
        at = GW * g
        out_ref[:, at : at + GW] = ot_ref[g].astype(F32).T.astype(BF)
        for h in range(NH):
            for part in range(3):
                src = GW * h + HS * part
                to = WIDTH * part + at + HS * h
                wg_ref[:, to : to + HS] = w_ref[g, 0:12, src : src + HS]


def lay_out(ot, w):
    return pl.pallas_call(
        lay_out_kernel,
        out_shape=(
            jax.ShapeDtypeStruct((BLK, WIDTH), BF),
            jax.ShapeDtypeStruct((12, 3 * WIDTH), F32),
        ),
        in_specs=[pl.BlockSpec(memory_space=VMEM)] * 2,
        out_specs=[pl.BlockSpec(memory_space=VMEM)] * 2,
        name="lay_out",
    )(ot, w)


def shards(hidden, masked, clip_lengths, qkv_weight, cotangent):
    ot, w = main(clip_lengths, hidden, masked.reshape(1, BLK), cotangent, qkv_weight)
    return lay_out(ot, w)


def solution(mesh):
    in_specs = (
        P(("dp", "seq"), None),
        P(("dp", "seq")),
        P("dp", None),
        P(),
        P(("dp", "seq"), None),
    )
    out_specs = (P(("dp", "seq"), None), P(("dp", "seq"), None))
    return jax.shard_map(shards, mesh=mesh, in_specs=in_specs, out_specs=out_specs, check_vma=False)
```

```python
import functools

import jax
import jax.numpy as jnp
from jax import lax
from jax.experimental import pallas as pl
from jax.experimental.pallas import tpu as pltpu
from jax.sharding import PartitionSpec as P

MESH = pl.DeviceIdType.MESH
VMEM = pltpu.VMEM
BF = jnp.bfloat16
F32 = jnp.float32
HS = 64
NH = 3
GW = NH * HS
BLK = 256
HALF = 4 * BLK
D = 1536
WIDTH = 768
NEG = -1e30
SCALE = 0.125
LIMIT = 62 * 1024 * 1024
STEPS = (1, 2, 3)


def mod4(v):
    return lax.rem(v, 4)


def dot(a, b):
    return jnp.dot(a, b, preferred_element_type=F32)


def dot_nt(a, b):
    return lax.dot_general(a, b, (((1,), (1,)), ((), ())), preferred_element_type=F32)


def lanes(at, size):
    return pl.ds(pl.multiple_of(at, size), size)


def main_kernel(
    len_ref, hidden_ref, mask_ref, cot_ref, w_ref,
    oland, r3a, r3b,
    land, wbuf, usend, ut, kvsend, kv, kvt, qsend, qland, qz, uz, nt, s_scr, p_scr, g_scr,
    qg, own, zsend, zland, osend, gbuf, theirs, mine, s1a, r1a, s1b, r1b, s5a, r5a, s5b, r5b, s3a, s3b, mx,
    wsem, hs, hr, as_, ar, ps, pr, ks, kr, us, ur, zs, zr, osm, orm, cs, cr, ds, dr, xs, xr,
):
    dp = lax.axis_index("dp")
    sq = lax.axis_index("seq")
    core, y, zl = lax.rem(dp, 2), lax.rem(dp // 2, 4), dp // 8
    x, zh = lax.rem(sq, 4), sq // 4
    z = zh * 2 + zl

    def dev(x, y, z, core):
        return ((lax.rem(z, 2) * 4 + y) * 2 + core, (z // 2) * 4 + x)

    xd = [dev(mod4(x + d), y, z, core) for d in STEPS]
    yd = [dev(x, mod4(y + d), z, core) for d in STEPS]
    zd = [dev(x, y, mod4(z + d), core) for d in STEPS]
    cp = dev(x, y, z, 1 - core)
    yzd = []
    for a in range(4):
        for b in range(4):
            if (a, b) != (0, 0):
                yy, zz = mod4(y + a), mod4(z + b)
                yzd.append((dev(x, yy, zz, core), yy * 4 + zz))
    zp = zd[1]
    right, far, left = xd
    def rcopy(src, dst, ss, rs, to):
        return pltpu.make_async_remote_copy(
            src_ref=src, dst_ref=dst, send_sem=ss, recv_sem=rs, device_id=to, device_id_type=MESH
        )

    def wcopy(j):
        return pltpu.make_async_copy(w_ref.at[:, WIDTH * j : WIDTH * (j + 1)], wbuf.at[j], wsem.at[j])

    for j in (1, 2, 0):
        wcopy(j).start()

    barrier = pltpu.get_barrier_semaphore()
    partners = [cp] + xd + [to for to, _ in yzd]
    for p in partners:
        pl.semaphore_signal(barrier, inc=1, device_id=p, device_id_type=MESH)

    half = BLK // 2
    top, bot = pl.ds(0, half), pl.ds(half, half)
    a0 = rcopy(hidden_ref.at[top], land.at[0, top], hs.at[0], hr.at[0], right)
    a1 = rcopy(hidden_ref.at[bot], land.at[1, bot], hs.at[1], hr.at[1], left)
    a2 = rcopy(hidden_ref.at[bot], land.at[0, bot], hs.at[2], hr.at[2], right)
    a3 = rcopy(hidden_ref.at[top], land.at[1, top], hs.at[3], hr.at[3], left)
    b0 = rcopy(land.at[0, top], land.at[2, top], hs.at[4], hr.at[4], right)
    b1 = rcopy(land.at[1, bot], land.at[2, bot], hs.at[5], hr.at[5], left)

    def slot(xb):
        return jnp.where(zh == 0, xb, 3 - xb)

    def turn(c):
        t = jnp.where(zh == 0, c, 7 - c)
        for h in range(NH):
            kvt[h, :, lanes(t * BLK, BLK)] = kv[c, h].T

    def kvcopy(c, xb):
        return rcopy(kv.at[c], kv.at[c], ks.at[xb], kr.at[xb], zp)

    def normalize(h):
        h = h.astype(F32)
        scale = lax.rsqrt(jnp.mean(h * h, axis=1, keepdims=True) + 1e-06)
        return (h * scale).astype(BF)

    def keep_turned(normed, xb):
        turned = normed.T
        for j in range(8):
            for par in range(2):
                at = 192 * j + 96 * par
                nt[par, 96 * j : 96 * (j + 1), lanes(xb * BLK, BLK)] = turned[at : at + 96, :]

    def arrive(xb):
        theirs = (1 - zh) * 4 + xb
        kvcopy(theirs, xb).wait_recv()
        turn(theirs)

    def group_copies(src, dst, ss, rs):
        return [rcopy(src.at[mod4(x + d)], dst, ss.at[i], rs.at[i], xd[i]) for i, d in enumerate(STEPS)]

    qz[...] = jnp.zeros_like(qz)
    uz[...] = jnp.zeros_like(uz)
    normed = normalize(hidden_ref[...])
    wcopy(1).wait()
    k = dot(normed, wbuf[1]).astype(BF)
    wcopy(2).wait()
    v = dot(normed, wbuf[2]).astype(BF)
    for g in range(4):
        for i in range(NH):
            cols = slice(GW * g + HS * i, GW * g + HS * (i + 1))
            kvsend[g, i] = jnp.concatenate([k[:, cols], v[:, cols]], axis=1)
    pl.semaphore_wait(barrier, len(partners))
    mine_c = zh * 4 + x
    kvx = group_copies(kvsend, kv.at[mine_c], as_, ar)
    for i in (1, 0, 2):
        kvx[i].start()
    kv[mine_c] = kvsend[x]
    kvcopy(mine_c, x).start()
    wcopy(0).wait()
    q = (dot(normed, wbuf[0]).astype(BF).astype(F32) * SCALE).T.astype(BF)
    for g in range(4):
        qsend[g] = q[GW * g : GW * (g + 1), :]
    qx = group_copies(qsend, qland.at[x], ps, pr)
    for i in (1, 0, 2):
        qx[i].start()
    qland[x] = qsend[x]
    keep = mask_ref[...] == 1
    for g in range(4):
        u = cot_ref[:, GW * g : GW * (g + 1)].astype(F32).T
        usend[g] = jnp.where(keep, u, 0.0).astype(BF)
    ux = group_copies(usend, ut.at[x], us, ur)
    for i in (1, 0, 2):
        ux[i].start()
    ut[x] = usend[x]
    keep_turned(normed, x)
    turn(mine_c)
    for i, d in ((0, 3), (2, 1), (1, 2)):
        kvx[i].wait_recv()
        xb = mod4(x + d)
        kvcopy(zh * 4 + xb, xb).start()
        turn(zh * 4 + xb)
    arrive(x)
    for c in qx:
        c.wait_recv()
    for c in (a0, a1, a2, a3):
        c.start()
    for xb in range(4):
        for i in range(NH):
            qz[i, 0:HS, lanes(slot(xb) * BLK, BLK)] = qland[xb, HS * i : HS * (i + 1), :]
    for c in ux:
        c.wait_recv()
    for xb in range(4):
        for i in range(NH):
            uz[i, HS : 2 * HS, lanes(slot(xb) * BLK, BLK)] = ut[xb, HS * i : HS * (i + 1), :]
    for c in kvx + qx + ux:
        c.wait_send()

    def zcopy(h, part):
        return rcopy(zsend.at[h, part], zland.at[h, part], zs.at[h, part], zr.at[h, part], zp)

    s1, r1, s5, r5, s3, r3 = (s1a, s1b), (r1a, r1b), (s5a, s5b), (r5a, r5b), (s3a, s3b), (r3a, r3b)

    def ccopy(n):
        return rcopy(s1[n], r1[n], cs.at[n], cr.at[n], cp)

    def ocopy(h, i):
        rows = pl.ds(pl.multiple_of(h * HS, HS), HS)
        return rcopy(osend.at[h, mod4(x + STEPS[i])], oland.at[x, rows], osm.at[h, i], orm.at[h, i], xd[i])

    def gather_grads(h):
        gbuf[h, 0:HS, :] = qg[h]
        for part in range(2):
            zcopy(h, part).wait()
            gbuf[h, HS * (part + 1) : HS * (part + 2), :] = (own[h, part] + zland[h, part].astype(F32)).astype(BF)

    def product(par, heads, blocks):
        total = None
        for xb in blocks:
            at_ = lanes(xb * BLK, BLK)
            g = jnp.concatenate([gbuf[h, :, at_] for h in heads], axis=0)
            p = dot_nt(nt[par, :, at_], g)
            total = p if total is None else total + p
        return total

    def dcopy(n, i):
        to, place = yzd[i]
        return rcopy(s5[n].at[place], r5[n].at[i], ds.at[n, i], dr.at[n, i], to)

    def to_yz(n, own_part):
        ccopy(n).wait()
        both = (own_part + r1[n][...].astype(F32)).astype(BF)
        for l in range(2):
            for yy in range(4):
                for u in range(2):
                    row = 384 * l + 96 * yy + 48 * u
                    s5[n][yy * 4 + 2 * u + l] = both[row : row + 48, :]
        for i in range(15):
            dcopy(n, i).start()

    def xcopy(n, i):
        return rcopy(s3[n].at[mod4(x + STEPS[i])], r3[n].at[x], xs.at[n, i], xr.at[n, i], xd[i])

    def to_x(n, width):
        t = s5[n][y * 4 + z].astype(F32)
        for i in range(15):
            dcopy(n, i).wait()
            t = t + r5[n][i].astype(F32)
        for xb in range(4):
            s3[n][xb, 0:12, 0:width] = t[12 * xb : 12 * (xb + 1), :]
        for i in range(3):
            xcopy(n, i).start()
        r3[n][x] = s3[n][x]

    e0 = len_ref[0, 0]
    e1 = e0 + len_ref[0, 1]

    def segment(pos):
        return (pos >= e0).astype(jnp.int32) + (pos >= e1).astype(jnp.int32)

    def key_block(t):
        return jnp.where(zh == 0, t, 7 - t)

    def slots(t):
        return range(max(0, t - 4), 4)

    def qpos(j):
        return zh * HALF + BLK * jnp.where(zh == 0, j, 3 - j)

    qsegs = [segment(qpos(j) + lax.broadcasted_iota(jnp.int32, (1, BLK), 1)) for j in range(4)]

    def at(j):
        return slice(BLK * j, BLK * (j + 1))

    def scores(h, steps):
        for t in steps:
            c = key_block(t)
            kseg = segment(c * BLK + lax.broadcasted_iota(jnp.int32, (BLK, 1), 0))
            for j in slots(t):
                s = dot(kv[c, h], qz[h, :, at(j)])
                s = jnp.where(kseg == qsegs[j], s, NEG)
                s_scr[at(t), at(j)] = s
                m = jnp.max(s, axis=0, keepdims=True)
                mx[0:1, at(j)] = m if t == 0 else jnp.maximum(mx[0:1, at(j)], m)

    def head(h, carry):
        scores(h, range(4, 8))

        ms = [mx[0:1, at(j)] for j in range(4)]
        ts = [jnp.zeros((1, BLK), F32) for _ in range(4)]
        for t in range(8):
            c = key_block(t)
            for j in slots(t):
                p = jnp.exp(s_scr[at(t), at(j)] - ms[j])
                ts[j] = ts[j] + jnp.sum(p, axis=0, keepdims=True)
                p_scr[at(t), at(j)] = p.astype(BF)
                s_scr[at(t), at(j)] = dot(kv[c, h], uz[h, :, at(j)])

        rts = [1.0 / ts[j] for j in range(4)]
        us_ = [uz[h, HS : 2 * HS, at(j)].astype(F32) for j in range(4)]
        urs = [(us_[j] * rts[j]).astype(BF) for j in range(4)]
        qrs = [(qz[h, 0:HS, at(j)].astype(F32) * rts[j]).astype(BF) for j in range(4)]

        def put(t, part, g):
            if t >= 4:
                zsend[h, part, :, lanes(jnp.where(zh == 0, t - 4, 7 - t) * BLK, BLK)] = g.astype(BF)
            else:
                own[h, part, :, lanes(jnp.where(zh == 0, t, 3 - t) * BLK, BLK)] = g

        def value_grad(t):
            g = jnp.zeros((HS, BLK), F32)
            for j in slots(t):
                g = g + dot_nt(urs[j], p_scr[at(t), at(j)])
            put(t, 1, g)

        def key_grad(t):
            g = jnp.zeros((HS, BLK), F32)
            for j in slots(t):
                ds_ = p_scr[at(t), at(j)].astype(F32) * (s_scr[at(t), at(j)] - deltas[j])
                ds_ = ds_.astype(BF)
                g_scr[at(t), at(j)] = ds_
                g = g + dot_nt(qrs[j], ds_)
            put(t, 0, g)

        for t in (7, 6, 5, 4):
            value_grad(t)
        zcopy(h, 1).start()

        deltas = []
        for j in range(4):
            rows = slice(0, BLK * (5 + j))
            o = (dot(kvt[h, HS : 2 * HS, rows], p_scr[rows, at(j)]) / ts[j]).astype(BF)
            osend[h, jnp.where(zh == 0, j, 3 - j)] = o
            deltas.append(jnp.sum(us_[j] * o.astype(F32), axis=0, keepdims=True))
        oland[x, pl.ds(pl.multiple_of(h * HS, HS), HS), :] = osend[h, x]

        for t in (7, 6, 5, 4):
            key_grad(t)
        zcopy(h, 0).start()

        for t in (3, 2, 1, 0):
            value_grad(t)
            key_grad(t)
        for j in range(4):
            rows = slice(0, BLK * (5 + j))
            g = dot(kvt[h, 0:HS, rows], g_scr[rows, at(j)]) * (rts[j] * SCALE)
            qg[h, :, lanes(jnp.where(zh == 0, j, 3 - j) * BLK, BLK)] = g.astype(BF)

        @pl.when(h == 0)
        def _():
            a0.wait_recv()
            b0.start()
            a1.wait_recv()
            b1.start()

        @pl.when(h == 1)
        def _():
            a2.wait_recv()
            keep_turned(normalize(land[0]), mod4(x + 3))
            a3.wait_recv()
            keep_turned(normalize(land[1]), mod4(x + 1))

        @pl.when(h < NH - 1)
        def _():
            scores(h + 1, range(4))

        return carry

    scores(0, range(4))
    for d in (3, 1, 2):
        arrive(mod4(x + d))
    for xb in range(4):
        kvcopy(zh * 4 + xb, xb).wait_send()
    lax.fori_loop(0, NH, head, 0)
    near, last = (x, mod4(x + 1), mod4(x + 3)), (mod4(x + 2),)
    gather_grads(0)
    gather_grads(1)
    theirs[...] = product(1 - core, (0, 1), near)
    mine[...] = product(core, (0, 1), near)
    b0.wait_recv()
    b1.wait_recv()
    keep_turned(normalize(land[2]), mod4(x + 2))
    s1a[...] = (theirs[...] + product(1 - core, (0, 1), last)).astype(BF)
    ccopy(0).start()
    for c in (a0, a1, a2, a3, b0, b1):
        c.wait_send()
    for h in range(NH):
        for i in range(3):
            ocopy(h, i).start()
    mine[...] += product(core, (0, 1), last)
    gather_grads(2)
    s1b[...] = product(1 - core, (2,), near + last).astype(BF)
    ccopy(1).start()
    to_yz(0, mine[...])
    to_yz(1, product(core, (2,), near + last))
    to_x(0, 2 * GW)
    to_x(1, GW)
    for h in range(NH):
        for i in range(3):
            ocopy(h, i).wait()
    for n in range(2):
        for i in range(3):
            xcopy(n, i).wait()


def main(lengths, hidden, mask, cot, w):
    dma = pltpu.SemaphoreType.DMA
    return pl.pallas_call(
        main_kernel,
        out_shape=(
            jax.ShapeDtypeStruct((4, GW, BLK), BF),
            jax.ShapeDtypeStruct((4, 16, 2 * GW), F32),
            jax.ShapeDtypeStruct((4, 16, 256), F32),
        ),
        in_specs=[pl.BlockSpec(memory_space=pltpu.SMEM)]
        + [pl.BlockSpec(memory_space=VMEM)] * 3
        + [pl.BlockSpec(memory_space=pl.ANY)],
        out_specs=[pl.BlockSpec(memory_space=VMEM)] * 3,
        scratch_shapes=[
            VMEM((3, BLK, D), BF),
            VMEM((3, D, WIDTH), BF),
            VMEM((4, GW, BLK), BF),
            VMEM((4, GW, BLK), BF),
            VMEM((4, NH, BLK, 2 * HS), BF),
            VMEM((8, NH, BLK, 2 * HS), BF),
            VMEM((NH, 2 * HS, 8 * BLK), BF),
            VMEM((4, GW, BLK), BF),
            VMEM((4, GW, BLK), BF),
            VMEM((NH, 2 * HS, HALF), BF),
            VMEM((NH, 2 * HS, HALF), BF),
            VMEM((2, WIDTH, HALF), BF),
            VMEM((8 * BLK, HALF), F32),
            VMEM((8 * BLK, HALF), BF),
            VMEM((8 * BLK, HALF), BF),
            VMEM((NH, HS, HALF), BF),
            VMEM((NH, 2, HS, HALF), F32),
            VMEM((NH, 2, HS, HALF), BF),
            VMEM((NH, 2, HS, HALF), BF),
            VMEM((NH, 4, HS, BLK), BF),
            VMEM((NH, GW, HALF), BF),
            VMEM((WIDTH, 2 * GW), F32),
            VMEM((WIDTH, 2 * GW), F32),
            VMEM((WIDTH, 2 * GW), BF),
            VMEM((WIDTH, 2 * GW), BF),
            VMEM((WIDTH, GW), BF),
            VMEM((WIDTH, GW), BF),
            VMEM((16, 48, 2 * GW), BF),
            VMEM((15, 48, 2 * GW), BF),
            VMEM((16, 48, GW), BF),
            VMEM((15, 48, GW), BF),
            VMEM((4, 16, 2 * GW), F32),
            VMEM((4, 16, 256), F32),
            VMEM((8, HALF), F32),
            dma((3,)), dma((6,)), dma((6,)), dma((3,)), dma((3,)), dma((3,)), dma((3,)),
            dma((4,)), dma((4,)), dma((3,)), dma((3,)),
            dma((NH, 2)), dma((NH, 2)), dma((NH, 3)), dma((NH, 3)), dma((2,)), dma((2,)),
            dma((2, 15)), dma((2, 15)), dma((2, 3)), dma((2, 3)),
        ],
        compiler_params=pltpu.CompilerParams(collective_id=0, has_side_effects=True, vmem_limit_bytes=LIMIT),
        name="main",
    )(lengths, hidden, mask, cot, w)


def lay_out_kernel(ot_ref, wa_ref, wb_ref, out_ref, wg_ref):
    for g in range(4):
        at = GW * g
        out_ref[:, at : at + GW] = ot_ref[g].astype(F32).T.astype(BF)
        for h in range(NH):
            for part in range(3):
                src = (GW * h if h < 2 else 0) + HS * part
                to = WIDTH * part + at + HS * h
                wg_ref[:, to : to + HS] = (wa_ref if h < 2 else wb_ref)[g, 0:12, src : src + HS]


def lay_out(ot, wa, wb):
    return pl.pallas_call(
        lay_out_kernel,
        out_shape=(
            jax.ShapeDtypeStruct((BLK, WIDTH), BF),
            jax.ShapeDtypeStruct((12, 3 * WIDTH), F32),
        ),
        in_specs=[pl.BlockSpec(memory_space=VMEM)] * 3,
        out_specs=[pl.BlockSpec(memory_space=VMEM)] * 2,
        name="lay_out",
    )(ot, wa, wb)


def shards(hidden, masked, clip_lengths, qkv_weight, cotangent):
    return lay_out(*main(clip_lengths, hidden, masked.reshape(1, BLK), cotangent, qkv_weight))


def solution(mesh):
    in_specs = (
        P(("dp", "seq"), None),
        P(("dp", "seq")),
        P("dp", None),
        P(),
        P(("dp", "seq"), None),
    )
    out_specs = (P(("dp", "seq"), None), P(("dp", "seq"), None))
    return jax.shard_map(shards, mesh=mesh, in_specs=in_specs, out_specs=out_specs, check_vma=False)
```

```python
import functools

import jax
import jax.numpy as jnp
from jax import lax
from jax.experimental import pallas as pl
from jax.experimental.pallas import tpu as pltpu
from jax.sharding import PartitionSpec as P

MESH = pl.DeviceIdType.MESH
VMEM = pltpu.VMEM
BF = jnp.bfloat16
F32 = jnp.float32
HS = 64
NH = 3
GW = NH * HS
BLK = 256
HALF = 4 * BLK
D = 1536
WIDTH = 768
NEG = -1e30
SCALE = 0.125
LIMIT = 62 * 1024 * 1024
STEPS = (1, 2, 3)


def mod4(v):
    return lax.rem(v, 4)


def dot(a, b):
    return jnp.dot(a, b, preferred_element_type=F32)


def dot_nt(a, b):
    return lax.dot_general(a, b, (((1,), (1,)), ((), ())), preferred_element_type=F32)


def lanes(at, size):
    return pl.ds(pl.multiple_of(at, size), size)


def main_kernel(
    len_ref, hidden_ref, mask_ref, cot_ref, w_ref,
    oland, r3a, r3b,
    land, wbuf, usend, ut, kvsend, kv, kvt, qsend, qland, qz, uz, nt, s_scr, p_scr, g_scr,
    qg, own, zsend, zland, osend, gbuf, theirs, mine, s1a, r1a, s1b, r1b, s2y, r2y, s4y, r4y, s2z, r2z, s4z, r4z, s5, r5, s3a, s3b, mx,
    wsem, hs, hr, as_, ar, ps, pr, ks, kr, us, ur, zs, zr, osm, orm, cs, cr, ts_, tr_, ds, dr, xs, xr,
):
    dp = lax.axis_index("dp")
    sq = lax.axis_index("seq")
    core, y, zl = lax.rem(dp, 2), lax.rem(dp // 2, 4), dp // 8
    x, zh = lax.rem(sq, 4), sq // 4
    z = zh * 2 + zl

    def dev(x, y, z, core):
        return ((lax.rem(z, 2) * 4 + y) * 2 + core, (z // 2) * 4 + x)

    xd = [dev(mod4(x + d), y, z, core) for d in STEPS]
    yd = [dev(x, mod4(y + d), z, core) for d in STEPS]
    zd = [dev(x, y, mod4(z + d), core) for d in STEPS]
    cp = dev(x, y, z, 1 - core)
    yzd = []
    for a in range(4):
        for b in range(4):
            if (a, b) != (0, 0):
                yy, zz = mod4(y + a), mod4(z + b)
                yzd.append((dev(x, yy, zz, core), yy * 4 + zz))
    zp = zd[1]
    right, far, left = xd
    def rcopy(src, dst, ss, rs, to):
        return pltpu.make_async_remote_copy(
            src_ref=src, dst_ref=dst, send_sem=ss, recv_sem=rs, device_id=to, device_id_type=MESH
        )

    def wcopy(j):
        return pltpu.make_async_copy(w_ref.at[:, WIDTH * j : WIDTH * (j + 1)], wbuf.at[j], wsem.at[j])

    for j in (1, 2, 0):
        wcopy(j).start()

    barrier = pltpu.get_barrier_semaphore()
    partners = [cp] + xd + [to for to, _ in yzd]
    for p in partners:
        pl.semaphore_signal(barrier, inc=1, device_id=p, device_id_type=MESH)

    half = BLK // 2
    top, bot = pl.ds(0, half), pl.ds(half, half)
    a0 = rcopy(hidden_ref.at[top], land.at[0, top], hs.at[0], hr.at[0], right)
    a1 = rcopy(hidden_ref.at[bot], land.at[1, bot], hs.at[1], hr.at[1], left)
    a2 = rcopy(hidden_ref.at[bot], land.at[0, bot], hs.at[2], hr.at[2], right)
    a3 = rcopy(hidden_ref.at[top], land.at[1, top], hs.at[3], hr.at[3], left)
    b0 = rcopy(land.at[0, top], land.at[2, top], hs.at[4], hr.at[4], right)
    b1 = rcopy(land.at[1, bot], land.at[2, bot], hs.at[5], hr.at[5], left)

    def slot(xb):
        return jnp.where(zh == 0, xb, 3 - xb)

    def turn(c):
        t = jnp.where(zh == 0, c, 7 - c)
        for h in range(NH):
            kvt[h, :, lanes(t * BLK, BLK)] = kv[c, h].T

    def kvcopy(c, xb):
        return rcopy(kv.at[c], kv.at[c], ks.at[xb], kr.at[xb], zp)

    def normalize(h):
        h = h.astype(F32)
        scale = lax.rsqrt(jnp.mean(h * h, axis=1, keepdims=True) + 1e-06)
        return (h * scale).astype(BF)

    def keep_turned(normed, xb):
        turned = normed.T
        for j in range(8):
            for par in range(2):
                at = 192 * j + 96 * par
                nt[par, 96 * j : 96 * (j + 1), lanes(xb * BLK, BLK)] = turned[at : at + 96, :]

    def arrive(xb):
        theirs = (1 - zh) * 4 + xb
        kvcopy(theirs, xb).wait_recv()
        turn(theirs)

    def group_copies(src, dst, ss, rs):
        return [rcopy(src.at[mod4(x + d)], dst, ss.at[i], rs.at[i], xd[i]) for i, d in enumerate(STEPS)]

    qz[...] = jnp.zeros_like(qz)
    uz[...] = jnp.zeros_like(uz)
    normed = normalize(hidden_ref[...])
    wcopy(1).wait()
    k = dot(normed, wbuf[1]).astype(BF)
    wcopy(2).wait()
    v = dot(normed, wbuf[2]).astype(BF)
    for g in range(4):
        for i in range(NH):
            cols = slice(GW * g + HS * i, GW * g + HS * (i + 1))
            kvsend[g, i] = jnp.concatenate([k[:, cols], v[:, cols]], axis=1)
    pl.semaphore_wait(barrier, len(partners))
    mine_c = zh * 4 + x
    kvx = group_copies(kvsend, kv.at[mine_c], as_, ar)
    for i in (1, 0, 2):
        kvx[i].start()
    kv[mine_c] = kvsend[x]
    kvcopy(mine_c, x).start()
    wcopy(0).wait()
    q = (dot(normed, wbuf[0]).astype(BF).astype(F32) * SCALE).T.astype(BF)
    for g in range(4):
        qsend[g] = q[GW * g : GW * (g + 1), :]
    qx = group_copies(qsend, qland.at[x], ps, pr)
    for i in (1, 0, 2):
        qx[i].start()
    qland[x] = qsend[x]
    keep = mask_ref[...] == 1
    for g in range(4):
        u = cot_ref[:, GW * g : GW * (g + 1)].astype(F32).T
        usend[g] = jnp.where(keep, u, 0.0).astype(BF)
    ux = group_copies(usend, ut.at[x], us, ur)
    for i in (1, 0, 2):
        ux[i].start()
    ut[x] = usend[x]
    keep_turned(normed, x)
    turn(mine_c)
    for i, d in ((0, 3), (2, 1), (1, 2)):
        kvx[i].wait_recv()
        xb = mod4(x + d)
        kvcopy(zh * 4 + xb, xb).start()
        turn(zh * 4 + xb)
    arrive(x)
    for c in qx:
        c.wait_recv()
    for c in (a0, a1, a2, a3):
        c.start()
    for xb in range(4):
        for i in range(NH):
            qz[i, 0:HS, lanes(slot(xb) * BLK, BLK)] = qland[xb, HS * i : HS * (i + 1), :]

    def zcopy(h, part):
        return rcopy(zsend.at[h, part], zland.at[h, part], zs.at[h, part], zr.at[h, part], zp)

    s1, r1, s3, r3 = (s1a, s1b), (r1a, r1b), (s3a, s3b), (r3a, r3b)

    def ccopy(n):
        return rcopy(s1[n], r1[n], cs.at[n], cr.at[n], cp)

    def ocopy(h, i):
        rows = pl.ds(pl.multiple_of(h * HS, HS), HS)
        return rcopy(osend.at[h, mod4(x + STEPS[i])], oland.at[x, rows], osm.at[h, i], orm.at[h, i], xd[i])

    def gather_grads(h):
        gbuf[h, 0:HS, :] = qg[h]
        for part in range(2):
            zcopy(h, part).wait()
            gbuf[h, HS * (part + 1) : HS * (part + 2), :] = (own[h, part] + zland[h, part].astype(F32)).astype(BF)

    def product(par, heads, blocks):
        total = None
        for xb in blocks:
            at_ = lanes(xb * BLK, BLK)
            g = jnp.concatenate([gbuf[h, :, at_] for h in heads], axis=0)
            p = dot_nt(nt[par, :, at_], g)
            total = p if total is None else total + p
        return total

    def stage(n, i):
        to = (yd, zd, zd, yd)[n][i]
        me = (y, z, z, y)[n]
        src, dst = ((s2y, r2y), (s2z, r2z), (s4y, r4y), (s4z, r4z))[n]
        return rcopy(src.at[mod4(me + STEPS[i])], dst.at[i], ts_.at[n, i], tr_.at[n, i], to)

    def places():
        for l in range(2):
            for yy in range(4):
                for u in range(2):
                    row = 384 * l + 96 * yy + 48 * u
                    yield yy, 2 * u + l, slice(row, row + 48)

    def first_stage():
        ccopy(0).wait()
        both = (mine[...] + r1a[...].astype(F32)).astype(BF)
        for yy, zz, rows in places():
            s2y[yy, zz] = both[rows, 0:256]
        for i in range(3):
            stage(0, i).start()
        for yy, zz, rows in places():
            s2z[zz, yy] = both[rows, 256 : 2 * GW]
        for i in range(3):
            stage(1, i).start()

    def stage_sum(n, src, dst, at_):
        t = src[at_].astype(F32)
        for i in range(3):
            stage(n, i).wait()
            t = t + dst[i].astype(F32)
        return t

    def second_stage():
        s4y[...] = stage_sum(0, s2y, r2y, y).astype(BF)
        for i in range(3):
            stage(2, i).start()
        s4z[...] = stage_sum(1, s2z, r2z, z).astype(BF)
        for i in range(3):
            stage(3, i).start()

    def dcopy(i):
        to, place = yzd[i]
        return rcopy(s5.at[place], r5.at[i], ds.at[i], dr.at[i], to)

    def to_yz(own_part):
        ccopy(1).wait()
        both = (own_part + r1b[...].astype(F32)).astype(BF)
        for yy, zz, rows in places():
            s5[yy * 4 + zz] = both[rows, :]
        for i in range(15):
            dcopy(i).start()

    def xcopy(n, i):
        return rcopy(s3[n].at[mod4(x + STEPS[i])], r3[n].at[x], xs.at[n, i], xr.at[n, i], xd[i])

    def to_x(n, columns):
        for xb in range(4):
            for t, first in columns:
                s3[n][xb, 0:12, first : first + t.shape[1]] = t[12 * xb : 12 * (xb + 1), :]
        for i in range(3):
            xcopy(n, i).start()
        r3[n][x] = s3[n][x]

    e0 = len_ref[0, 0]
    e1 = e0 + len_ref[0, 1]

    def segment(pos):
        return (pos >= e0).astype(jnp.int32) + (pos >= e1).astype(jnp.int32)

    def key_block(t):
        return jnp.where(zh == 0, t, 7 - t)

    def slots(t):
        return range(max(0, t - 4), 4)

    def qpos(j):
        return zh * HALF + BLK * jnp.where(zh == 0, j, 3 - j)

    qsegs = [segment(qpos(j) + lax.broadcasted_iota(jnp.int32, (1, BLK), 1)) for j in range(4)]

    def at(j):
        return slice(BLK * j, BLK * (j + 1))

    def scores(h, steps):
        for t in steps:
            c = key_block(t)
            kseg = segment(c * BLK + lax.broadcasted_iota(jnp.int32, (BLK, 1), 0))
            for j in slots(t):
                s = dot(kv[c, h], qz[h, :, at(j)])
                s = jnp.where(kseg == qsegs[j], s, NEG)
                s_scr[at(t), at(j)] = s
                m = jnp.max(s, axis=0, keepdims=True)
                mx[0:1, at(j)] = m if t == 0 else jnp.maximum(mx[0:1, at(j)], m)

    def head(h, carry):
        scores(h, range(4, 8))

        ms = [mx[0:1, at(j)] for j in range(4)]
        ts = [jnp.zeros((1, BLK), F32) for _ in range(4)]
        for t in range(8):
            c = key_block(t)
            for j in slots(t):
                p = jnp.exp(s_scr[at(t), at(j)] - ms[j])
                ts[j] = ts[j] + jnp.sum(p, axis=0, keepdims=True)
                p_scr[at(t), at(j)] = p.astype(BF)
                s_scr[at(t), at(j)] = dot(kv[c, h], uz[h, :, at(j)])

        rts = [1.0 / ts[j] for j in range(4)]
        us_ = [uz[h, HS : 2 * HS, at(j)].astype(F32) for j in range(4)]
        urs = [(us_[j] * rts[j]).astype(BF) for j in range(4)]
        qrs = [(qz[h, 0:HS, at(j)].astype(F32) * rts[j]).astype(BF) for j in range(4)]

        def put(t, part, g):
            if t >= 4:
                zsend[h, part, :, lanes(jnp.where(zh == 0, t - 4, 7 - t) * BLK, BLK)] = g.astype(BF)
            else:
                own[h, part, :, lanes(jnp.where(zh == 0, t, 3 - t) * BLK, BLK)] = g

        def value_grad(t):
            g = jnp.zeros((HS, BLK), F32)
            for j in slots(t):
                g = g + dot_nt(urs[j], p_scr[at(t), at(j)])
            put(t, 1, g)

        def key_grad(t):
            g = jnp.zeros((HS, BLK), F32)
            for j in slots(t):
                ds_ = p_scr[at(t), at(j)].astype(F32) * (s_scr[at(t), at(j)] - deltas[j])
                ds_ = ds_.astype(BF)
                g_scr[at(t), at(j)] = ds_
                g = g + dot_nt(qrs[j], ds_)
            put(t, 0, g)

        for t in (7, 6, 5, 4):
            value_grad(t)
        zcopy(h, 1).start()

        deltas = []
        for j in range(4):
            rows = slice(0, BLK * (5 + j))
            o = (dot(kvt[h, HS : 2 * HS, rows], p_scr[rows, at(j)]) / ts[j]).astype(BF)
            osend[h, jnp.where(zh == 0, j, 3 - j)] = o
            deltas.append(jnp.sum(us_[j] * o.astype(F32), axis=0, keepdims=True))
        oland[x, pl.ds(pl.multiple_of(h * HS, HS), HS), :] = osend[h, x]

        for t in (7, 6, 5, 4):
            key_grad(t)
        zcopy(h, 0).start()

        for t in (3, 2, 1, 0):
            value_grad(t)
            key_grad(t)
        for j in range(4):
            rows = slice(0, BLK * (5 + j))
            g = dot(kvt[h, 0:HS, rows], g_scr[rows, at(j)]) * (rts[j] * SCALE)
            qg[h, :, lanes(jnp.where(zh == 0, j, 3 - j) * BLK, BLK)] = g.astype(BF)

        @pl.when(h == 0)
        def _():
            a0.wait_recv()
            b0.start()
            a1.wait_recv()
            b1.start()

        @pl.when(h == 1)
        def _():
            a2.wait_recv()
            keep_turned(normalize(land[0]), mod4(x + 3))
            a3.wait_recv()
            keep_turned(normalize(land[1]), mod4(x + 1))

        @pl.when(h < NH - 1)
        def _():
            scores(h + 1, range(4))

        return carry

    scores(0, range(4))
    for c in ux:
        c.wait_recv()
    for xb in range(4):
        for i in range(NH):
            uz[i, HS : 2 * HS, lanes(slot(xb) * BLK, BLK)] = ut[xb, HS * i : HS * (i + 1), :]
    for d in (3, 1, 2):
        arrive(mod4(x + d))
    for xb in range(4):
        kvcopy(zh * 4 + xb, xb).wait_send()
    for c in kvx + qx + ux:
        c.wait_send()
    lax.fori_loop(0, NH, head, 0)
    near, last = (x, mod4(x + 1), mod4(x + 3)), (mod4(x + 2),)
    gather_grads(0)
    gather_grads(1)
    theirs[...] = product(1 - core, (0, 1), near)
    mine[...] = product(core, (0, 1), near)
    b0.wait_recv()
    b1.wait_recv()
    keep_turned(normalize(land[2]), mod4(x + 2))
    s1a[...] = (theirs[...] + product(1 - core, (0, 1), last)).astype(BF)
    ccopy(0).start()
    for c in (a0, a1, a2, a3, b0, b1):
        c.wait_send()
    for h in range(NH):
        for i in range(3):
            ocopy(h, i).start()
    mine[...] += product(core, (0, 1), last)
    gather_grads(2)
    s1b[...] = product(1 - core, (2,), near + last).astype(BF)
    ccopy(1).start()
    first_stage()
    to_yz(product(core, (2,), near + last))
    second_stage()
    to_x(0, [(stage_sum(2, s4y, r4y, z), 0), (stage_sum(3, s4z, r4z, y), 256)])
    t = s5[y * 4 + z].astype(F32)
    for i in range(15):
        dcopy(i).wait()
        t = t + r5[i].astype(F32)
    to_x(1, [(t, 0)])
    for h in range(NH):
        for i in range(3):
            ocopy(h, i).wait()
    for n in range(2):
        for i in range(3):
            xcopy(n, i).wait()


def main(lengths, hidden, mask, cot, w):
    dma = pltpu.SemaphoreType.DMA
    return pl.pallas_call(
        main_kernel,
        out_shape=(
            jax.ShapeDtypeStruct((4, GW, BLK), BF),
            jax.ShapeDtypeStruct((4, 16, 2 * GW), F32),
            jax.ShapeDtypeStruct((4, 16, 256), F32),
        ),
        in_specs=[pl.BlockSpec(memory_space=pltpu.SMEM)]
        + [pl.BlockSpec(memory_space=VMEM)] * 3
        + [pl.BlockSpec(memory_space=pl.ANY)],
        out_specs=[pl.BlockSpec(memory_space=VMEM)] * 3,
        scratch_shapes=[
            VMEM((3, BLK, D), BF),
            VMEM((3, D, WIDTH), BF),
            VMEM((4, GW, BLK), BF),
            VMEM((4, GW, BLK), BF),
            VMEM((4, NH, BLK, 2 * HS), BF),
            VMEM((8, NH, BLK, 2 * HS), BF),
            VMEM((NH, 2 * HS, 8 * BLK), BF),
            VMEM((4, GW, BLK), BF),
            VMEM((4, GW, BLK), BF),
            VMEM((NH, 2 * HS, HALF), BF),
            VMEM((NH, 2 * HS, HALF), BF),
            VMEM((2, WIDTH, HALF), BF),
            VMEM((8 * BLK, HALF), F32),
            VMEM((8 * BLK, HALF), BF),
            VMEM((8 * BLK, HALF), BF),
            VMEM((NH, HS, HALF), BF),
            VMEM((NH, 2, HS, HALF), F32),
            VMEM((NH, 2, HS, HALF), BF),
            VMEM((NH, 2, HS, HALF), BF),
            VMEM((NH, 4, HS, BLK), BF),
            VMEM((NH, GW, HALF), BF),
            VMEM((WIDTH, 2 * GW), F32),
            VMEM((WIDTH, 2 * GW), F32),
            VMEM((WIDTH, 2 * GW), BF),
            VMEM((WIDTH, 2 * GW), BF),
            VMEM((WIDTH, GW), BF),
            VMEM((WIDTH, GW), BF),
            VMEM((4, 4, 48, 256), BF),
            VMEM((3, 4, 48, 256), BF),
            VMEM((4, 48, 256), BF),
            VMEM((3, 48, 256), BF),
            VMEM((4, 4, 48, 128), BF),
            VMEM((3, 4, 48, 128), BF),
            VMEM((4, 48, 128), BF),
            VMEM((3, 48, 128), BF),
            VMEM((16, 48, GW), BF),
            VMEM((15, 48, GW), BF),
            VMEM((4, 16, 2 * GW), F32),
            VMEM((4, 16, 256), F32),
            VMEM((8, HALF), F32),
            dma((3,)), dma((6,)), dma((6,)), dma((3,)), dma((3,)), dma((3,)), dma((3,)),
            dma((4,)), dma((4,)), dma((3,)), dma((3,)),
            dma((NH, 2)), dma((NH, 2)), dma((NH, 3)), dma((NH, 3)), dma((2,)), dma((2,)),
            dma((4, 3)), dma((4, 3)), dma((15,)), dma((15,)), dma((2, 3)), dma((2, 3)),
        ],
        compiler_params=pltpu.CompilerParams(collective_id=0, has_side_effects=True, vmem_limit_bytes=LIMIT),
        name="main",
    )(lengths, hidden, mask, cot, w)


def lay_out_kernel(ot_ref, wa_ref, wb_ref, out_ref, wg_ref):
    for g in range(4):
        at = GW * g
        out_ref[:, at : at + GW] = ot_ref[g].astype(F32).T.astype(BF)
        for h in range(NH):
            for part in range(3):
                src = (GW * h if h < 2 else 0) + HS * part
                to = WIDTH * part + at + HS * h
                wg_ref[:, to : to + HS] = (wa_ref if h < 2 else wb_ref)[g, 0:12, src : src + HS]


def lay_out(ot, wa, wb):
    return pl.pallas_call(
        lay_out_kernel,
        out_shape=(
            jax.ShapeDtypeStruct((BLK, WIDTH), BF),
            jax.ShapeDtypeStruct((12, 3 * WIDTH), F32),
        ),
        in_specs=[pl.BlockSpec(memory_space=VMEM)] * 3,
        out_specs=[pl.BlockSpec(memory_space=VMEM)] * 2,
        name="lay_out",
    )(ot, wa, wb)


def shards(hidden, masked, clip_lengths, qkv_weight, cotangent):
    return lay_out(*main(clip_lengths, hidden, masked.reshape(1, BLK), cotangent, qkv_weight))


def solution(mesh):
    in_specs = (
        P(("dp", "seq"), None),
        P(("dp", "seq")),
        P("dp", None),
        P(),
        P(("dp", "seq"), None),
    )
    out_specs = (P(("dp", "seq"), None), P(("dp", "seq"), None))
    return jax.shard_map(shards, mesh=mesh, in_specs=in_specs, out_specs=out_specs, check_vma=False)
```

```python
import functools

import jax
import jax.numpy as jnp
from jax import lax
from jax.experimental import pallas as pl
from jax.experimental.pallas import tpu as pltpu
from jax.sharding import PartitionSpec as P

MESH = pl.DeviceIdType.MESH
VMEM = pltpu.VMEM
BF = jnp.bfloat16
F32 = jnp.float32
HS = 64
NH = 3
GW = NH * HS
CA = 2 * GW + HS
CB = 2 * HS
BLK = 256
HALF = 4 * BLK
D = 1536
WIDTH = 768
NEG = -1e30
SCALE = 0.125
LIMIT = 62 * 1024 * 1024
STEPS = (1, 2, 3)


def mod4(v):
    return lax.rem(v, 4)


def dot(a, b):
    return jnp.dot(a, b, preferred_element_type=F32)


def dot_nt(a, b):
    return lax.dot_general(a, b, (((1,), (1,)), ((), ())), preferred_element_type=F32)


def lanes(at, size):
    return pl.ds(pl.multiple_of(at, size), size)


def main_kernel(
    len_ref, hidden_ref, mask_ref, cot_ref, w_ref,
    oland, r3a, r3b,
    land, wbuf, usend, ut, kvsend, kv, kvt, qsend, qland, qz, uz, nt, s_scr, p_scr, g_scr,
    qg, own, zsend, zland, osend, gbuf, theirs, mine, s1a, r1a, s1b, r1b, s2y, r2y, s4y, r4y, s2z, r2z, s4z, r4z, s5, r5, s3a, s3b, mx,
    wsem, hs, hr, as_, ar, ps, pr, ks, kr, us, ur, zs, zr, osm, orm, cs, cr, ts_, tr_, ds, dr, xs, xr,
):
    dp = lax.axis_index("dp")
    sq = lax.axis_index("seq")
    core, y, zl = lax.rem(dp, 2), lax.rem(dp // 2, 4), dp // 8
    x, zh = lax.rem(sq, 4), sq // 4
    z = zh * 2 + zl

    def dev(x, y, z, core):
        return ((lax.rem(z, 2) * 4 + y) * 2 + core, (z // 2) * 4 + x)

    xd = [dev(mod4(x + d), y, z, core) for d in STEPS]
    yd = [dev(x, mod4(y + d), z, core) for d in STEPS]
    zd = [dev(x, y, mod4(z + d), core) for d in STEPS]
    cp = dev(x, y, z, 1 - core)
    yzd = []
    for a in range(4):
        for b in range(4):
            if (a, b) != (0, 0):
                yy, zz = mod4(y + a), mod4(z + b)
                yzd.append((dev(x, yy, zz, core), yy * 4 + zz))
    zp = zd[1]
    right, far, left = xd
    def rcopy(src, dst, ss, rs, to):
        return pltpu.make_async_remote_copy(
            src_ref=src, dst_ref=dst, send_sem=ss, recv_sem=rs, device_id=to, device_id_type=MESH
        )

    def wcopy(j):
        return pltpu.make_async_copy(w_ref.at[:, WIDTH * j : WIDTH * (j + 1)], wbuf.at[j], wsem.at[j])

    for j in (1, 2, 0):
        wcopy(j).start()

    barrier = pltpu.get_barrier_semaphore()
    partners = [cp] + xd + [to for to, _ in yzd]
    for p in partners:
        pl.semaphore_signal(barrier, inc=1, device_id=p, device_id_type=MESH)

    half = BLK // 2
    top, bot = pl.ds(0, half), pl.ds(half, half)
    a0 = rcopy(hidden_ref.at[top], land.at[0, top], hs.at[0], hr.at[0], right)
    a1 = rcopy(hidden_ref.at[bot], land.at[1, bot], hs.at[1], hr.at[1], left)
    a2 = rcopy(hidden_ref.at[bot], land.at[0, bot], hs.at[2], hr.at[2], right)
    a3 = rcopy(hidden_ref.at[top], land.at[1, top], hs.at[3], hr.at[3], left)
    b0 = rcopy(land.at[0, top], land.at[2, top], hs.at[4], hr.at[4], right)
    b1 = rcopy(land.at[1, bot], land.at[2, bot], hs.at[5], hr.at[5], left)

    def slot(xb):
        return jnp.where(zh == 0, xb, 3 - xb)

    def turn(c):
        t = jnp.where(zh == 0, c, 7 - c)
        for h in range(NH):
            kvt[h, :, lanes(t * BLK, BLK)] = kv[c, h].T

    def kvcopy(c, xb):
        return rcopy(kv.at[c], kv.at[c], ks.at[xb], kr.at[xb], zp)

    def normalize(h):
        h = h.astype(F32)
        scale = lax.rsqrt(jnp.mean(h * h, axis=1, keepdims=True) + 1e-06)
        return (h * scale).astype(BF)

    def keep_turned(normed, xb):
        turned = normed.T
        for j in range(8):
            for par in range(2):
                at = 192 * j + 96 * par
                nt[par, 96 * j : 96 * (j + 1), lanes(xb * BLK, BLK)] = turned[at : at + 96, :]

    def arrive(xb):
        theirs = (1 - zh) * 4 + xb
        kvcopy(theirs, xb).wait_recv()
        turn(theirs)

    def group_copies(src, dst, ss, rs):
        return [rcopy(src.at[mod4(x + d)], dst, ss.at[i], rs.at[i], xd[i]) for i, d in enumerate(STEPS)]

    qz[...] = jnp.zeros_like(qz)
    uz[...] = jnp.zeros_like(uz)
    normed = normalize(hidden_ref[...])
    wcopy(1).wait()
    k = dot(normed, wbuf[1]).astype(BF)
    wcopy(2).wait()
    v = dot(normed, wbuf[2]).astype(BF)
    for g in range(4):
        for i in range(NH):
            cols = slice(GW * g + HS * i, GW * g + HS * (i + 1))
            kvsend[g, i] = jnp.concatenate([k[:, cols], v[:, cols]], axis=1)
    pl.semaphore_wait(barrier, len(partners))
    mine_c = zh * 4 + x
    kvx = group_copies(kvsend, kv.at[mine_c], as_, ar)
    for i in (1, 0, 2):
        kvx[i].start()
    kv[mine_c] = kvsend[x]
    kvcopy(mine_c, x).start()
    wcopy(0).wait()
    q = (dot(normed, wbuf[0]).astype(BF).astype(F32) * SCALE).T.astype(BF)
    for g in range(4):
        qsend[g] = q[GW * g : GW * (g + 1), :]
    qx = group_copies(qsend, qland.at[x], ps, pr)
    for i in (1, 0, 2):
        qx[i].start()
    qland[x] = qsend[x]
    keep = mask_ref[...] == 1
    for g in range(4):
        u = cot_ref[:, GW * g : GW * (g + 1)].astype(F32).T
        usend[g] = jnp.where(keep, u, 0.0).astype(BF)
    ux = group_copies(usend, ut.at[x], us, ur)
    for i in (1, 0, 2):
        ux[i].start()
    ut[x] = usend[x]
    keep_turned(normed, x)
    turn(mine_c)
    for i, d in ((0, 3), (2, 1), (1, 2)):
        kvx[i].wait_recv()
        xb = mod4(x + d)
        kvcopy(zh * 4 + xb, xb).start()
        turn(zh * 4 + xb)
    arrive(x)
    for c in qx:
        c.wait_recv()
    for c in (a0, a1, a2, a3):
        c.start()
    for xb in range(4):
        for i in range(NH):
            qz[i, 0:HS, lanes(slot(xb) * BLK, BLK)] = qland[xb, HS * i : HS * (i + 1), :]

    def zcopy(h, part):
        return rcopy(zsend.at[h, part], zland.at[h, part], zs.at[h, part], zr.at[h, part], zp)

    s1, r1, s3, r3 = (s1a, s1b), (r1a, r1b), (s3a, s3b), (r3a, r3b)

    def ccopy(n):
        return rcopy(s1[n], r1[n], cs.at[n], cr.at[n], cp)

    def ocopy(h, i):
        rows = pl.ds(pl.multiple_of(h * HS, HS), HS)
        return rcopy(osend.at[h, mod4(x + STEPS[i])], oland.at[x, rows], osm.at[h, i], orm.at[h, i], xd[i])

    def gather_grads(h):
        gbuf[h, 0:HS, :] = qg[h]
        for part in range(2):
            zcopy(h, part).wait()
            gbuf[h, HS * (part + 1) : HS * (part + 2), :] = (own[h, part] + zland[h, part].astype(F32)).astype(BF)

    def product(par, n, blocks):
        total = None
        for xb in blocks:
            at_ = lanes(xb * BLK, BLK)
            if n == 0:
                g = jnp.concatenate([gbuf[0, :, at_], gbuf[1, :, at_], qg[2, :, at_]], axis=0)
            else:
                g = gbuf[2, HS:GW, at_]
            p = dot_nt(nt[par, :, at_], g)
            total = p if total is None else total + p
        return total

    def stage(n, i):
        to = (yd, zd, zd, yd)[n][i]
        me = (y, z, z, y)[n]
        src, dst = ((s2y, r2y), (s2z, r2z), (s4y, r4y), (s4z, r4z))[n]
        return rcopy(src.at[mod4(me + STEPS[i])], dst.at[i], ts_.at[n, i], tr_.at[n, i], to)

    def places():
        for l in range(2):
            for yy in range(4):
                for u in range(2):
                    row = 384 * l + 96 * yy + 48 * u
                    yield yy, 2 * u + l, slice(row, row + 48)

    def first_stage():
        ccopy(0).wait()
        both = (mine[...] + r1a[...].astype(F32)).astype(BF)
        for yy, zz, rows in places():
            s2y[yy, zz] = both[rows, 0:256]
        for i in range(3):
            stage(0, i).start()
        for yy, zz, rows in places():
            s2z[zz, yy] = both[rows, 256:CA]
        for i in range(3):
            stage(1, i).start()

    def stage_sum(n, src, dst, at_):
        t = src[at_].astype(F32)
        for i in range(3):
            stage(n, i).wait()
            t = t + dst[i].astype(F32)
        return t

    def second_stage():
        s4y[...] = stage_sum(0, s2y, r2y, y).astype(BF)
        for i in range(3):
            stage(2, i).start()
        s4z[...] = stage_sum(1, s2z, r2z, z).astype(BF)
        for i in range(3):
            stage(3, i).start()

    def dcopy(i):
        to, place = yzd[i]
        return rcopy(s5.at[place], r5.at[i], ds.at[i], dr.at[i], to)

    def to_yz(own_part):
        ccopy(1).wait()
        both = (own_part + r1b[...].astype(F32)).astype(BF)
        for yy, zz, rows in places():
            s5[yy * 4 + zz] = both[rows, :]
        for i in range(15):
            dcopy(i).start()

    def xcopy(n, i):
        return rcopy(s3[n].at[mod4(x + STEPS[i])], r3[n].at[x], xs.at[n, i], xr.at[n, i], xd[i])

    def to_x(n, columns):
        for xb in range(4):
            for t, first in columns:
                s3[n][xb, 0:12, first : first + t.shape[1]] = t[12 * xb : 12 * (xb + 1), :]
        for i in range(3):
            xcopy(n, i).start()
        r3[n][x] = s3[n][x]

    e0 = len_ref[0, 0]
    e1 = e0 + len_ref[0, 1]

    def segment(pos):
        return (pos >= e0).astype(jnp.int32) + (pos >= e1).astype(jnp.int32)

    def key_block(t):
        return jnp.where(zh == 0, t, 7 - t)

    def slots(t):
        return range(max(0, t - 4), 4)

    def qpos(j):
        return zh * HALF + BLK * jnp.where(zh == 0, j, 3 - j)

    qsegs = [segment(qpos(j) + lax.broadcasted_iota(jnp.int32, (1, BLK), 1)) for j in range(4)]

    def at(j):
        return slice(BLK * j, BLK * (j + 1))

    def scores(h, steps):
        for t in steps:
            c = key_block(t)
            kseg = segment(c * BLK + lax.broadcasted_iota(jnp.int32, (BLK, 1), 0))
            for j in slots(t):
                s = dot(kv[c, h], qz[h, :, at(j)])
                s = jnp.where(kseg == qsegs[j], s, NEG)
                s_scr[at(t), at(j)] = s
                m = jnp.max(s, axis=0, keepdims=True)
                mx[0:1, at(j)] = m if t == 0 else jnp.maximum(mx[0:1, at(j)], m)

    def head(h, carry):
        scores(h, range(4, 8))

        ms = [mx[0:1, at(j)] for j in range(4)]
        ts = [jnp.zeros((1, BLK), F32) for _ in range(4)]
        for t in range(8):
            c = key_block(t)
            for j in slots(t):
                p = jnp.exp(s_scr[at(t), at(j)] - ms[j])
                ts[j] = ts[j] + jnp.sum(p, axis=0, keepdims=True)
                p_scr[at(t), at(j)] = p.astype(BF)
                s_scr[at(t), at(j)] = dot(kv[c, h], uz[h, :, at(j)])

        rts = [1.0 / ts[j] for j in range(4)]
        us_ = [uz[h, HS : 2 * HS, at(j)].astype(F32) for j in range(4)]
        urs = [(us_[j] * rts[j]).astype(BF) for j in range(4)]
        qrs = [(qz[h, 0:HS, at(j)].astype(F32) * rts[j]).astype(BF) for j in range(4)]

        def put(t, part, g):
            if t >= 4:
                zsend[h, part, :, lanes(jnp.where(zh == 0, t - 4, 7 - t) * BLK, BLK)] = g.astype(BF)
            else:
                own[h, part, :, lanes(jnp.where(zh == 0, t, 3 - t) * BLK, BLK)] = g

        def value_grad(t):
            g = jnp.zeros((HS, BLK), F32)
            for j in slots(t):
                g = g + dot_nt(urs[j], p_scr[at(t), at(j)])
            put(t, 1, g)

        def key_grad(t):
            g = jnp.zeros((HS, BLK), F32)
            for j in slots(t):
                ds_ = p_scr[at(t), at(j)].astype(F32) * (s_scr[at(t), at(j)] - deltas[j])
                ds_ = ds_.astype(BF)
                g_scr[at(t), at(j)] = ds_
                g = g + dot_nt(qrs[j], ds_)
            put(t, 0, g)

        for t in (7, 6, 5, 4):
            value_grad(t)
        zcopy(h, 1).start()

        deltas = []
        for j in range(4):
            rows = slice(0, BLK * (5 + j))
            o = (dot(kvt[h, HS : 2 * HS, rows], p_scr[rows, at(j)]) / ts[j]).astype(BF)
            osend[h, jnp.where(zh == 0, j, 3 - j)] = o
            deltas.append(jnp.sum(us_[j] * o.astype(F32), axis=0, keepdims=True))
        oland[x, pl.ds(pl.multiple_of(h * HS, HS), HS), :] = osend[h, x]

        for t in (7, 6, 5, 4):
            key_grad(t)
        zcopy(h, 0).start()

        for t in (3, 2, 1, 0):
            value_grad(t)
            key_grad(t)
        for j in range(4):
            rows = slice(0, BLK * (5 + j))
            g = dot(kvt[h, 0:HS, rows], g_scr[rows, at(j)]) * (rts[j] * SCALE)
            qg[h, :, lanes(jnp.where(zh == 0, j, 3 - j) * BLK, BLK)] = g.astype(BF)

        @pl.when(h == 0)
        def _():
            a0.wait_recv()
            b0.start()
            a1.wait_recv()
            b1.start()

        @pl.when(h == 1)
        def _():
            a2.wait_recv()
            keep_turned(normalize(land[0]), mod4(x + 3))
            a3.wait_recv()
            keep_turned(normalize(land[1]), mod4(x + 1))

        @pl.when(h < NH - 1)
        def _():
            scores(h + 1, range(4))

        return carry

    scores(0, range(4))
    for c in ux:
        c.wait_recv()
    for xb in range(4):
        for i in range(NH):
            uz[i, HS : 2 * HS, lanes(slot(xb) * BLK, BLK)] = ut[xb, HS * i : HS * (i + 1), :]
    for d in (3, 1, 2):
        arrive(mod4(x + d))
    for xb in range(4):
        kvcopy(zh * 4 + xb, xb).wait_send()
    for c in kvx + qx + ux:
        c.wait_send()
    lax.fori_loop(0, NH, head, 0)
    near, last = (x, mod4(x + 1), mod4(x + 3)), (mod4(x + 2),)
    gather_grads(0)
    gather_grads(1)
    theirs[...] = product(1 - core, 0, near)
    mine[...] = product(core, 0, near)
    b0.wait_recv()
    b1.wait_recv()
    keep_turned(normalize(land[2]), mod4(x + 2))
    s1a[...] = (theirs[...] + product(1 - core, 0, last)).astype(BF)
    ccopy(0).start()
    for c in (a0, a1, a2, a3, b0, b1):
        c.wait_send()
    for h in range(NH):
        for i in range(3):
            ocopy(h, i).start()
    mine[...] += product(core, 0, last)
    first_stage()
    gather_grads(2)
    s1b[...] = product(1 - core, 1, near + last).astype(BF)
    ccopy(1).start()
    to_yz(product(core, 1, near + last))
    second_stage()
    to_x(0, [(stage_sum(2, s4y, r4y, z), 0), (stage_sum(3, s4z, r4z, y), 256)])
    t = s5[y * 4 + z].astype(F32)
    for i in range(15):
        dcopy(i).wait()
        t = t + r5[i].astype(F32)
    to_x(1, [(t, 0)])
    for h in range(NH):
        for i in range(3):
            ocopy(h, i).wait()
    for n in range(2):
        for i in range(3):
            xcopy(n, i).wait()


def main(lengths, hidden, mask, cot, w):
    dma = pltpu.SemaphoreType.DMA
    return pl.pallas_call(
        main_kernel,
        out_shape=(
            jax.ShapeDtypeStruct((4, GW, BLK), BF),
            jax.ShapeDtypeStruct((4, 16, CA), F32),
            jax.ShapeDtypeStruct((4, 16, CB), F32),
        ),
        in_specs=[pl.BlockSpec(memory_space=pltpu.SMEM)]
        + [pl.BlockSpec(memory_space=VMEM)] * 3
        + [pl.BlockSpec(memory_space=pl.ANY)],
        out_specs=[pl.BlockSpec(memory_space=VMEM)] * 3,
        scratch_shapes=[
            VMEM((3, BLK, D), BF),
            VMEM((3, D, WIDTH), BF),
            VMEM((4, GW, BLK), BF),
            VMEM((4, GW, BLK), BF),
            VMEM((4, NH, BLK, 2 * HS), BF),
            VMEM((8, NH, BLK, 2 * HS), BF),
            VMEM((NH, 2 * HS, 8 * BLK), BF),
            VMEM((4, GW, BLK), BF),
            VMEM((4, GW, BLK), BF),
            VMEM((NH, 2 * HS, HALF), BF),
            VMEM((NH, 2 * HS, HALF), BF),
            VMEM((2, WIDTH, HALF), BF),
            VMEM((8 * BLK, HALF), F32),
            VMEM((8 * BLK, HALF), BF),
            VMEM((8 * BLK, HALF), BF),
            VMEM((NH, HS, HALF), BF),
            VMEM((NH, 2, HS, HALF), F32),
            VMEM((NH, 2, HS, HALF), BF),
            VMEM((NH, 2, HS, HALF), BF),
            VMEM((NH, 4, HS, BLK), BF),
            VMEM((NH, GW, HALF), BF),
            VMEM((WIDTH, CA), F32),
            VMEM((WIDTH, CA), F32),
            VMEM((WIDTH, CA), BF),
            VMEM((WIDTH, CA), BF),
            VMEM((WIDTH, CB), BF),
            VMEM((WIDTH, CB), BF),
            VMEM((4, 4, 48, 256), BF),
            VMEM((3, 4, 48, 256), BF),
            VMEM((4, 48, 256), BF),
            VMEM((3, 48, 256), BF),
            VMEM((4, 4, 48, CA - 256), BF),
            VMEM((3, 4, 48, CA - 256), BF),
            VMEM((4, 48, CA - 256), BF),
            VMEM((3, 48, CA - 256), BF),
            VMEM((16, 48, CB), BF),
            VMEM((15, 48, CB), BF),
            VMEM((4, 16, CA), F32),
            VMEM((4, 16, CB), F32),
            VMEM((8, HALF), F32),
            dma((3,)), dma((6,)), dma((6,)), dma((3,)), dma((3,)), dma((3,)), dma((3,)),
            dma((4,)), dma((4,)), dma((3,)), dma((3,)),
            dma((NH, 2)), dma((NH, 2)), dma((NH, 3)), dma((NH, 3)), dma((2,)), dma((2,)),
            dma((4, 3)), dma((4, 3)), dma((15,)), dma((15,)), dma((2, 3)), dma((2, 3)),
        ],
        compiler_params=pltpu.CompilerParams(collective_id=0, has_side_effects=True, vmem_limit_bytes=LIMIT),
        name="main",
    )(lengths, hidden, mask, cot, w)


def lay_out_kernel(ot_ref, wa_ref, wb_ref, out_ref, wg_ref):
    for g in range(4):
        at = GW * g
        out_ref[:, at : at + GW] = ot_ref[g].astype(F32).T.astype(BF)
        for h in range(NH):
            for part in range(3):
                src = GW * h + HS * part
                to = WIDTH * part + at + HS * h
                if src < CA:
                    wg_ref[:, to : to + HS] = wa_ref[g, 0:12, src : src + HS]
                else:
                    wg_ref[:, to : to + HS] = wb_ref[g, 0:12, src - CA : src - CA + HS]


def lay_out(ot, wa, wb):
    return pl.pallas_call(
        lay_out_kernel,
        out_shape=(
            jax.ShapeDtypeStruct((BLK, WIDTH), BF),
            jax.ShapeDtypeStruct((12, 3 * WIDTH), F32),
        ),
        in_specs=[pl.BlockSpec(memory_space=VMEM)] * 3,
        out_specs=[pl.BlockSpec(memory_space=VMEM)] * 2,
        name="lay_out",
    )(ot, wa, wb)


def shards(hidden, masked, clip_lengths, qkv_weight, cotangent):
    return lay_out(*main(clip_lengths, hidden, masked.reshape(1, BLK), cotangent, qkv_weight))


def solution(mesh):
    in_specs = (
        P(("dp", "seq"), None),
        P(("dp", "seq")),
        P("dp", None),
        P(),
        P(("dp", "seq"), None),
    )
    out_specs = (P(("dp", "seq"), None), P(("dp", "seq"), None))
    return jax.shard_map(shards, mesh=mesh, in_specs=in_specs, out_specs=out_specs, check_vma=False)
```
